512 devices in a mesh: pulse: 4 (over y), tile: 32 (over z, core), row: 4 (over x).
Axes of the slice: x: 4, y: 4, z: 16, core: 2. Of those that a mesh axis runs over, the one named last changes fastest.
Arguments:
- raw_pulses: float32 [2, 8192, 8192], P(None, ('pulse', 'tile', 'row')), may hold values from -6 to 6
- range_weight: float32 [8192], replicated, may hold values from 0.25 to 1.75
- visibility: int32 [32, 512], replicated, may hold values from 0 to 1, as said below
- offsets: int32 [32, 512], replicated, may hold values from 0 to 60
- doppler_rate: int32 [32], replicated, may hold values from 1 to 4095
- phase_error: float32 [32, 16], replicated, may hold values from -3.140625 to 3.140625
- row_groups: int32 [512], replicated, may hold values from 0 to 15, never falling along the last dimension, each value on 1 to 64 neighbouring positions
Outputs:
- focused: float32 [32, 512, 1024], P('tile', ('pulse', 'row'))
The draws below stay inside these ranges and needn't reach their ends.
Inputs may be any that keep to these rules, and one draw needn't show every extreme that they name: `visibility`: write block b = (p * 32 + s) * 4 + w with p < 4, s < 32, w < 4. For every tile and every pair p, w, the tile sees at least 8 and at most 16 of the 32 blocks with that p and w; in every draw some tile sees exactly 16 of them for every p and w.
All inputs are finite; a program needn't handle non-finite values.
Results may differ from the reference program's by a relative error of at most 0.018.
Values may be sent and summed in bfloat16 or wider, within the bound.
A program may use at most 64 MiB of HBM per device.

```python
import math
import jax
import jax.numpy as jnp
import numpy as np
from jax import lax

NR = 8192
TILE_COLS = 512
TILE_ROWS = 512
UNIT = 128
PB = 16
GROUPS = 16
TILES = 32
BLOCKS = 512
PULSES = 8192
SUB = 128
N_PULSE = 4
N_TILE = 32
N_ROW = 4


def draw_visibility(key, part):
    key = jax.random.fold_in(key, 11)
    count_key, pick_key, order_key = jax.random.split(key, 3)
    half = N_TILE // 2
    least = max(1, N_TILE // 4)
    counts = jax.random.randint(count_key, (TILES, N_PULSE, 1, N_ROW), least, half + 1)
    chosen = jax.random.randint(pick_key, (), 0, TILES)
    tile_ids = jnp.arange(TILES, dtype=jnp.int32)[:, None, None, None]
    counts = jnp.where(tile_ids == chosen, half, counts)
    order_keys = jax.random.split(order_key, TILES * N_PULSE * N_ROW)
    ranks = jax.vmap(lambda k: jax.random.permutation(k, N_TILE))(order_keys)
    ranks = ranks.reshape(TILES, N_PULSE, N_ROW, N_TILE).transpose(0, 1, 3, 2)
    seen = (ranks < counts).astype(jnp.int32)
    return seen.reshape(TILES, BLOCKS)


def place_ends(array, rng, low, high):
    longest = array.shape.index(max(array.shape))
    spots = []
    for shift in (0, 1):
        where = [jax.random.randint(jax.random.fold_in(rng, axis), (), 0, length) for axis, length in enumerate(array.shape)]
        where[longest] = (where[longest] + shift) % array.shape[longest]
        spots.append(tuple(where))
    return array.at[spots[0]].set(low).at[spots[1]].set(high)


def block_levels(own_key, shape, cuts, smallest, high):
    loudness, own = 1.0, jax.random.fold_in(own_key, 6)
    for position, blocks in cuts:
        steps = jnp.exp(jax.random.uniform(jax.random.fold_in(own, position), (blocks,), jnp.float32, smallest / len(cuts), high / len(cuts)))
        loudness = loudness * jnp.repeat(steps, shape[position] // blocks).reshape([-1 if axis == position else 1 for axis in range(len(shape))])
    return loudness


def profile(count, total, reach, slope):
    loads = [(1 << 20) // math.isqrt(grade ** slope) + 1 for grade in range(2, count + 1)]
    spare, given = total - reach - (count - 1), [1] * (count - 1)
    while spare > 0:
        free = [i for i in range(count - 1) if given[i] < reach]
        whole, remaining = sum([loads[i] for i in free]), spare
        for i in free:
            addition = min(reach - given[i], max(1, remaining * loads[i] // whole), spare)
            given[i] = given[i] + addition
            spare = spare - addition
    return np.array([reach] + given)


def ragged(key, count, total, limit, skew):
    if count == 2:
        one = jax.random.randint(key, (), max(1, total - limit), min(limit, total - 1) + 1)
        return jnp.stack([one, total - one])
    tallies = jnp.asarray(profile(count, total, limit, skew), jnp.int32)
    pairs = (count - 1) // 2
    giver, sink = tallies[1:1 + 2 * pairs:2], tallies[2:2 + 2 * pairs:2]
    room = jnp.minimum(giver - 1, limit - sink)
    shifted = jax.random.randint(jax.random.fold_in(key, 1), (pairs,), 0, 1 << 20) % (room + 1)
    tallies = tallies.at[1:1 + 2 * pairs:2].set(giver - shifted).at[2:2 + 2 * pairs:2].set(sink + shifted)
    return tallies[jax.random.permutation(jax.random.fold_in(key, 2), count)]


def normal_values(rng, shape, spread, reach, cuts=(), held_as=jnp.bfloat16):
    values = spread * jax.random.normal(rng, shape, jnp.float32)
    if cuts:
        values = values * block_levels(rng, shape, cuts, -0.22, 0.18)
    return jnp.clip(values, -reach, reach).astype(held_as)


def setup_inputs(seed: int = 0) -> dict:
    key_of = jax.random.split(jax.random.key(seed), 8)
    return {
        "raw_pulses": normal_values(key_of[0], (2, PULSES, NR), 1.0, 6.0, ((1, 512),), jnp.float32),
        "range_weight": jnp.clip(1.0 + 0.15 * jax.random.normal(key_of[1], (NR,), jnp.float32), 0.25, 1.75),
        "visibility": draw_visibility(jax.random.fold_in(key_of[7], 71), 0),
        "offsets": place_ends(jax.random.randint(key_of[3], (TILES, BLOCKS), 0, (NR - TILE_COLS) // UNIT + 1), jax.random.fold_in(key_of[3], 1), 0, ((NR - TILE_COLS) // UNIT + 1) - 1).astype(jnp.int32),
        "doppler_rate": place_ends(jax.random.randint(key_of[4], (TILES,), 1, 4096), jax.random.fold_in(key_of[4], 1), 1, 4095).astype(jnp.int32),
        "phase_error": jnp.clip(jax.random.uniform(key_of[5], (TILES, GROUPS), jnp.float32, -3.140625, 3.140625), -3.140625, 3.140625),
        "row_groups": jnp.searchsorted(jnp.cumsum(ragged(key_of[6], GROUPS, TILE_ROWS, TILE_ROWS // 8, 1)), jnp.arange(TILE_ROWS), side="right").astype(jnp.int32),
    }


modulus = 4096
two_pi = 2.0 * math.pi

def phase_pair(row_ids, pulse_ids, rate):
    step_phase = pulse_ids * rate % modulus
    ticks = row_ids[:, None, None] * step_phase[None] % modulus
    angles = ticks.astype(jnp.float32) * (two_pi / modulus)
    cosine = jnp.cos(angles)
    sine = jnp.sin(angles)
    row_count = row_ids.shape[0]
    real_part = jnp.stack([cosine, -sine], axis=2).reshape(row_count, -1).astype(jnp.bfloat16)
    imag_part = jnp.stack([sine, cosine], axis=2).reshape(row_count, -1).astype(jnp.bfloat16)
    return (real_part, imag_part)

def focus_matrix(errors, groups, sub_rows):
    row_index = lax.broadcasted_iota(jnp.int32, (sub_rows, sub_rows), 0)
    col_index = lax.broadcasted_iota(jnp.int32, (sub_rows, sub_rows), 1)
    base_angle = (row_index * col_index % sub_rows).astype(jnp.float32) * (-two_pi / sub_rows)
    labels = jnp.arange(errors.shape[0], dtype=jnp.int32)
    row_phase = lax.optimization_barrier(jnp.sum(jnp.where(groups[:, None] == labels[None, :], errors[None, :], 0.0), axis=1))
    angles = base_angle + row_phase[None, :]
    norm_value = 1.0 / math.sqrt(sub_rows)
    return (jnp.cos(angles) * norm_value, jnp.sin(angles) * norm_value)

def complex_rows(mat_re, mat_im, field):
    width = field.shape[1] // 2
    field_re = field[:, :width]
    field_im = field[:, width:]
    hp = lax.Precision.HIGHEST
    out_re = jnp.dot(mat_re, field_re, precision=hp) - jnp.dot(mat_im, field_im, precision=hp)
    out_im = jnp.dot(mat_re, field_im, precision=hp) + jnp.dot(mat_im, field_re, precision=hp)
    return jnp.concatenate([out_re, out_im], axis=1)

def reference(raw_pulses, range_weight, visibility, offsets, doppler_rate, phase_error, row_groups):
    signal = raw_pulses[0] * range_weight + 1j * (raw_pulses[1] * range_weight)
    spectrum = jnp.fft.fft(signal, axis=-1) / math.sqrt(NR)
    compressed = jnp.stack([spectrum.real, spectrum.imag]).astype(jnp.bfloat16)
    pulse_offsets = jnp.arange(PB, dtype=jnp.int32)
    row_ids = jnp.arange(TILE_ROWS, dtype=jnp.int32)
    block_table = jnp.arange(BLOCKS, dtype=jnp.int32).reshape(-1, 16)

    def tile_image(tile_id):
        rate = doppler_rate[tile_id]
        seen_row = visibility[tile_id]
        offset_row = offsets[tile_id]

        def add_blocks(running, block_ids):

            def window_at(block_id):
                return lax.dynamic_slice(compressed, (jnp.int32(0), (block_id * PB).astype(jnp.int32), (offset_row[block_id] * UNIT).astype(jnp.int32)), (2, PB, TILE_COLS))
            windows = jax.vmap(window_at)(block_ids)
            windows = windows * seen_row[block_ids].astype(jnp.bfloat16)[:, None, None, None]
            stacked = windows.reshape(-1, TILE_COLS)
            phase_re, phase_im = phase_pair(row_ids, block_ids[:, None] * PB + pulse_offsets[None, :], rate)
            summed = jnp.concatenate([jnp.dot(phase_re, stacked, preferred_element_type=jnp.float32), jnp.dot(phase_im, stacked, preferred_element_type=jnp.float32)], axis=1)
            return (running + summed, None)
        start_value = jnp.zeros((TILE_ROWS, 2 * TILE_COLS), jnp.float32)
        image, unused = lax.scan(add_blocks, start_value, block_table)
        image = image * (1.0 / math.sqrt(PULSES))
        pieces = []
        for sub_index in range(N_PULSE):
            groups = row_groups[sub_index * SUB:(sub_index + 1) * SUB]
            mat_re, mat_im = focus_matrix(phase_error[tile_id], groups, SUB)
            pieces.append(complex_rows(mat_re, mat_im, image[sub_index * SUB:(sub_index + 1) * SUB]))
        return jnp.concatenate(pieces, axis=0)
    return lax.map(tile_image, jnp.arange(TILES, dtype=jnp.int32))
```

```python
from functools import partial
import math

import numpy as np
import jax
import jax.numpy as jnp
from jax import lax
from jax.experimental import pallas as pl
from jax.experimental.pallas import tpu as pltpu
from jax.sharding import PartitionSpec as P

MESH = pl.DeviceIdType.MESH
F32 = jnp.float32
BF16 = jnp.bfloat16
NSUB = 2

TWO_PI = 2.0 * math.pi


def dft_tables():
    n1, v = np.arange(128)[:, None], np.arange(128)[None, :]
    a = TWO_PI * (n1 * v % 128) / 128
    c, s = np.cos(a), np.sin(a)
    first = np.block([[c, -s], [s, c]]).astype(np.float32)
    n2 = np.arange(64)[:, None]
    t = TWO_PI * (n2 * v % 8192) / 8192
    twist = np.stack([np.cos(t), -np.sin(t)]).astype(np.float32)
    u = np.arange(64)[:, None]
    b = TWO_PI * (u * np.arange(64)[None, :] % 64) / 64
    second = np.concatenate([np.cos(b), np.sin(b)], axis=1).astype(np.float32)
    focus = np.block([[c, s], [-s, c]]).astype(np.float32)
    return first, twist, second, focus


def swap_bits(blocks, low):
    blocks = list(blocks)
    lane = lax.broadcasted_iota(jnp.int32, blocks[0].shape, 1)
    bit = 1
    while bit < len(blocks):
        shift = bit << low
        high = (lane & shift) != 0
        for i in range(len(blocks)):
            if i & bit == 0:
                a, b = blocks[i], blocks[i | bit]
                blocks[i] = jnp.where(high, pltpu.roll(b, shift, 1), a)
                blocks[i | bit] = jnp.where(high, b, pltpu.roll(a, 128 - shift, 1))
        bit *= 2
    return blocks


def unit_root(ticks, period):
    x = ticks.astype(F32) * (1.0 / period)
    x = x - jnp.where(x >= 0.5, 1.0, 0.0)
    h = x * math.pi
    q = h * h
    sh = h * (1.0 + q * (-1 / 6 + q * (1 / 120 + q * (-1 / 5040 + q * (1 / 362880)))))
    ch = 1.0 + q * (-1 / 2 + q * (1 / 24 + q * (-1 / 720 + q * (1 / 40320 + q * (-1 / 3628800)))))
    return 1.0 - 2.0 * sh * sh, 2.0 * sh * ch


def compress_kernel(x_ref, first_ref, twist_ref, second_ref, out_ref, mid, spec):
    hp = lax.Precision.HIGHEST
    x = jnp.concatenate([x_ref[0], x_ref[1]], axis=1)
    mid[...] = jnp.dot(x, first_ref[...], precision=hp, preferred_element_type=F32)
    t_re, t_im = twist_ref[0], twist_ref[1]
    norm = 1.0 / math.sqrt(8192)

    def pulse(j, carry):
        y = mid[pl.ds(pl.multiple_of(j * 64, 64), 64), :]
        y_re, y_im = y[:, :128], y[:, 128:]
        b_re = y_re * t_re - y_im * t_im
        b_im = y_re * t_im + y_im * t_re
        right = jnp.concatenate(
            [jnp.concatenate([b_re, b_im], axis=1), jnp.concatenate([b_im, -b_re], axis=1)], axis=0
        )
        z = jnp.dot(second_ref[...], right, precision=hp, preferred_element_type=F32) * norm
        spec[j] = z[:, :128]
        spec[j + 16] = z[:, 128:]
        return carry

    lax.fori_loop(0, 16, pulse, 0)

    def rows(g, carry):
        at = pl.ds(pl.multiple_of(g * 8, 8), 8)
        blocks = swap_bits([spec[i, at, :] for i in range(32)], 0)
        for i in range(32):
            spec[i, at, :] = blocks[i]
        return carry

    lax.fori_loop(0, 8, rows, 0)

    def cast(i, carry):
        out_ref[i] = spec[i].astype(BF16)
        return carry

    lax.fori_loop(0, 32, cast, 0)


def compress(signal, first, twist, second):
    return pl.pallas_call(
        compress_kernel,
        out_shape=jax.ShapeDtypeStruct((32, 64, 128), BF16),
        in_specs=[pl.BlockSpec(memory_space=pltpu.VMEM)] * 4,
        out_specs=pl.BlockSpec(memory_space=pltpu.VMEM),
        scratch_shapes=[pltpu.VMEM((1024, 256), F32), pltpu.VMEM((32, 64, 128), F32)],
        compiler_params=pltpu.CompilerParams(vmem_limit_bytes=40 * 2**20),
    )(signal, first, twist, second)


def image_kernel(
    rate_ref, msg_ref, spots_ref, error_ref, focus_ref, out_ref,
    recv, pick, gath, weight, phase, part_a, part_b, send_a, send_b, recv_a, recv_b, msg2, recv2,
    sem_s1, sem_r1, sem_sa, sem_ra, sem_sb, sem_rb, sem_s2, sem_r2,
):
    py = lax.axis_index("pulse")
    zc = lax.axis_index("tile")
    wx = lax.axis_index("row")
    z, core = zc // 2, zc % 2
    me = py * 8 + wx * 2 + core

    def slot_of(p, w, c):
        return (((p % 2) * 4 + w) * 2 + c) * 2 + p // 2

    own_slot = slot_of(py, wx, core)
    up = (py, ((z + 1) % 16) * 2 + core, wx)
    down = (py, ((z + 15) % 16) * 2 + core, wx)

    def to_peer(d):
        return (py + d // 8) % 4, (wx + (d // 2) % 4) % 4, (core + d % 2) % 2

    def from_peer(d):
        return (py + 4 - d // 8) % 4, (wx + 4 - (d // 2) % 4) % 4, (core + d % 2) % 2

    barrier = pltpu.get_barrier_semaphore()

    def greet(d, carry):
        p, w, c = to_peer(d)
        pl.semaphore_signal(barrier, inc=1, device_id=(p, z * 2 + c, w), device_id_type=MESH)
        return carry

    lax.fori_loop(1, 32, greet, 0)
    pl.semaphore_signal(barrier, inc=1, device_id=up, device_id_type=MESH)
    pl.semaphore_signal(barrier, inc=1, device_id=down, device_id_type=MESH)
    pl.semaphore_wait(barrier, 33)

    def first_copy(d):
        p, w, c = to_peer(d)
        return pltpu.make_async_remote_copy(
            src_ref=msg_ref.at[p * 8 + w * 2 + c],
            dst_ref=recv.at[own_slot],
            send_sem=sem_s1.at[d],
            recv_sem=sem_r1.at[own_slot],
            device_id=(p, z * 2 + c, w),
            device_id_type=MESH,
        )

    def first_arrival(d):
        p, w, c = from_peer(d)
        slot = slot_of(p, w, c)
        return pltpu.make_async_remote_copy(
            src_ref=msg_ref.at[0],
            dst_ref=recv.at[slot],
            send_sem=sem_s1.at[d],
            recv_sem=sem_r1.at[slot],
            device_id=(p, z * 2 + c, w),
            device_id_type=MESH,
        )

    def start_first(d, carry):
        first_copy(d).start()
        return carry

    lax.fori_loop(1, 32, start_first, 0)
    recv[own_slot] = msg_ref[me]

    def spots(i, carry):
        key = lax.broadcasted_iota(jnp.int32, (128, 256), 0)
        lane = lax.broadcasted_iota(jnp.int32, (128, 256), 1)
        chosen = jnp.where(key == i * 4 + lane // 64, 1.0, 0.0).astype(BF16)
        place = jnp.dot(spots_ref[...], chosen, preferred_element_type=F32)
        unit = (lax.broadcasted_iota(jnp.int32, (256, 256), 1) % 64).astype(F32)
        pick[i] = jnp.where(place == unit, 1.0, 0.0).astype(BF16)
        return carry

    lax.fori_loop(0, 8, spots, 0)

    def azimuth(t, carry):
        rate = rate_ref[t]
        low = lax.broadcasted_iota(jnp.int32, (8, 512), 0)
        row = lax.broadcasted_iota(jnp.int32, (8, 512), 1)
        step = (low * rate) & 4095
        a_re, a_im = unit_root((step * row) & 4095, 4096)
        b_re, b_im = unit_root((((step * 8) & 4095) * row) & 4095, 4096)
        for w in range(4):
            parts_re, parts_im = [], []
            for k in (2 * w, 2 * w + 1):
                k_re, k_im = b_re[k:k + 1, :], b_im[k:k + 1, :]
                parts_re.append(a_re * k_re - a_im * k_im)
                parts_im.append(a_re * k_im + a_im * k_re)
            e_re = jnp.concatenate(parts_re, axis=0)
            e_im = jnp.concatenate(parts_im, axis=0)
            weight[t, w * 32:w * 32 + 16, 0:512] = e_re.astype(BF16)
            weight[t, w * 32:w * 32 + 16, 512:1024] = e_im.astype(BF16)
            weight[t, w * 32 + 16:w * 32 + 32, 0:512] = (-e_im).astype(BF16)
            weight[t, w * 32 + 16:w * 32 + 32, 512:1024] = e_re.astype(BF16)
        sub = lax.broadcasted_iota(jnp.int32, (8, 128), 0)
        lane = lax.broadcasted_iota(jnp.int32, (8, 128), 1)
        for p2 in range(2):
            sigma = p2 * 32 + z * 2 + sub // 4
            s_re, s_im = unit_root((((sigma * rate) & 63) * lane) & 63, 64)
            phase[t, 2 * p2] = s_re
            phase[t, 2 * p2 + 1] = s_im
        return carry

    lax.fori_loop(0, 32, azimuth, 0)

    def await_first(d, carry):
        first_arrival(d).wait_recv()
        return carry

    lax.fori_loop(1, 32, await_first, 0)

    def gather(p2, carry):
        found = []
        for w in range(4):
            slot = pl.multiple_of((p2 * 4 + w) * 4, 4)
            data = recv[pl.ds(slot, 4)].reshape(256, 128)
            found.append(jnp.dot(pick[p2 * 4 + w], data, preferred_element_type=F32))
        for t in range(32):
            rows = slice(t * 8, t * 8 + 8)
            blocks = swap_bits([f[rows, :] for f in found], 5)
            for vi in range(4):
                gath[t, vi * 2 + p2] = blocks[vi]
        return carry

    lax.fori_loop(0, 2, gather, 0)

    def partial_image(dest, store):
        sub = lax.broadcasted_iota(jnp.int32, (8, 128), 0) < 4
        sums = []
        for k in range(2):
            t = dest * 2 + k
            left = gath[t].reshape(64, 128).astype(BF16)
            y = jnp.dot(left, weight[t], preferred_element_type=F32)
            s = [phase[t, i] for i in range(4)]
            mine = {}
            for g in range(4):
                for vi in range(4):
                    tot_re = tot_im = None
                    for p2 in range(2):
                        rows = slice((vi * 2 + p2) * 8, (vi * 2 + p2) * 8 + 8)
                        y_re = y[rows, g * 128:g * 128 + 128]
                        y_im = y[rows, 512 + g * 128:640 + g * 128]
                        r = y_re * s[2 * p2] - y_im * s[2 * p2 + 1]
                        i = y_re * s[2 * p2 + 1] + y_im * s[2 * p2]
                        tot_re = r if tot_re is None else tot_re + r
                        tot_im = i if tot_im is None else tot_im + i
                    mine[0, g, vi] = tot_re + pltpu.roll(tot_re, 4, 0)
                    mine[1, g, vi] = tot_im + pltpu.roll(tot_im, 4, 0)
            sums.append(mine)
        for ri in range(2):
            for g in range(4):
                for vi in range(4):
                    both = jnp.where(sub, sums[0][ri, g, vi], sums[1][ri, g, vi])
                    at = ri * 512 + g * 128
                    store[vi * 8:vi * 8 + 8, at:at + 128] = both

    rows_sub = 32 // NSUB

    def ring_copy(src, dst, send_sem, recv_sem, step, h, peer):
        rows = pl.ds(h * rows_sub, rows_sub)
        return pltpu.make_async_remote_copy(
            src_ref=src.at[step, rows, :],
            dst_ref=dst.at[step, rows, :],
            send_sem=send_sem.at[step, h],
            recv_sem=recv_sem.at[step, h],
            device_id=peer,
            device_id_type=MESH,
        )

    def copy_a(step, h):
        return ring_copy(send_a, recv_a, sem_sa, sem_ra, step, h, up)

    def copy_b(step, h):
        return ring_copy(send_b, recv_b, sem_sb, sem_rb, step, h, down)

    def ring_step(s, carry):
        partial_image((z + 8 - s) % 16, part_a)
        partial_image((z + 9 + s) % 16, part_b)

        @pl.when(s == 0)
        def _():
            send_a[0] = part_a[...].astype(BF16)
            send_b[0] = part_b[...].astype(BF16)
            for h in range(NSUB):
                copy_a(0, h).start()
                copy_b(0, h).start()

        @pl.when(s > 0)
        def _():
            for h in range(NSUB):
                rows = slice(h * rows_sub, (h + 1) * rows_sub)
                copy_a(s - 1, h).wait_recv()
                send_a[s, rows, :] = (part_a[rows, :] + recv_a[s - 1, rows, :].astype(F32)).astype(BF16)
                copy_a(s, h).start()

                copy_b(s - 1, h).wait_recv()
                send_b[s, rows, :] = (part_b[rows, :] + recv_b[s - 1, rows, :].astype(F32)).astype(BF16)

                @pl.when(s < 7)
                def _():
                    copy_b(s, h).start()
        return carry

    lax.fori_loop(0, 8, ring_step, 0)
    for h in range(NSUB):
        rows = slice(h * rows_sub, (h + 1) * rows_sub)
        copy_a(7, h).wait_recv()
        part_b[rows, :] = part_b[rows, :] + recv_b[6, rows, :].astype(F32) + recv_a[7, rows, :].astype(F32)

    rights = []
    for vi in range(4):
        for q in range(4):
            at = q * 128
            i_re = part_b[vi * 8:vi * 8 + 8, at:at + 128]
            i_im = part_b[vi * 8:vi * 8 + 8, 512 + at:640 + at]
            c, s = error_ref[0, :, at:at + 128], error_ref[1, :, at:at + 128]
            rights.append(jnp.concatenate([i_re * c - i_im * s, i_re * s + i_im * c], axis=1))
    right = (jnp.concatenate(rights, axis=0) * (1.0 / 1024)).astype(BF16)
    spun = lax.dot_general(
        focus_ref[...], right, (((1,), (1,)), ((), ())), preferred_element_type=F32
    )
    for w in range(4):
        blocks = []
        for i in range(8):
            at = (i // 4) * 128 + w * 32 + (i % 4) * 8
            blocks.append(spun[at:at + 8, :])
        blocks = swap_bits(blocks, 2)
        for i in range(8):
            msg2[(i // 2) * 8 + w * 2 + i % 2] = blocks[i]

    def last_copy(d):
        p, w, c = to_peer(d)
        return pltpu.make_async_remote_copy(
            src_ref=msg2.at[p * 8 + w * 2 + c],
            dst_ref=recv2.at[me],
            send_sem=sem_s2.at[d],
            recv_sem=sem_r2.at[me],
            device_id=(p, z * 2 + c, w),
            device_id_type=MESH,
        )

    def last_arrival(d):
        p, w, c = from_peer(d)
        k = p * 8 + w * 2 + c
        return pltpu.make_async_remote_copy(
            src_ref=msg2.at[0],
            dst_ref=recv2.at[k],
            send_sem=sem_s2.at[d],
            recv_sem=sem_r2.at[k],
            device_id=(p, z * 2 + c, w),
            device_id_type=MESH,
        )

    def start_last(d, carry):
        last_copy(d).start()
        return carry

    lax.fori_loop(1, 32, start_last, 0)
    recv2[me] = msg2[me]

    def finish_sends(d, carry):
        first_copy(d).wait_send()
        return carry

    lax.fori_loop(1, 32, finish_sends, 0)
    for s in range(8):
        for h in range(NSUB):
            copy_a(s, h).wait_send()
            if s < 7:
                copy_b(s, h).wait_send()

    def await_last(d, carry):
        last_arrival(d).wait_recv()
        return carry

    lax.fori_loop(1, 32, await_last, 0)
    blocks = swap_bits([recv2[k] for k in range(32)], 0)
    for i in range(32):
        ri, hi, unit = i // 16, (i // 4) % 4, i % 4
        at = ri * 512 + unit * 128
        out_ref[hi * 8:hi * 8 + 8, at:at + 128] = blocks[i]

    def finish_last(d, carry):
        last_copy(d).wait_send()
        return carry

    lax.fori_loop(1, 32, finish_last, 0)


def make_image(rates, messages, spots, errors, focus):
    vmem = pl.BlockSpec(memory_space=pltpu.VMEM)
    dma = pltpu.SemaphoreType.DMA
    return pl.pallas_call(
        image_kernel,
        out_shape=jax.ShapeDtypeStruct((32, 1024), F32),
        in_specs=[pl.BlockSpec(memory_space=pltpu.SMEM)] + [vmem] * 4,
        out_specs=vmem,
        scratch_shapes=[
            pltpu.VMEM((32, 64, 128), BF16),
            pltpu.VMEM((8, 256, 256), BF16),
            pltpu.VMEM((32, 8, 8, 128), F32),
            pltpu.VMEM((32, 128, 1024), BF16),
            pltpu.VMEM((32, 4, 8, 128), F32),
            pltpu.VMEM((32, 1024), F32),
            pltpu.VMEM((32, 1024), F32),
            pltpu.VMEM((8, 32, 1024), BF16),
            pltpu.VMEM((8, 32, 1024), BF16),
            pltpu.VMEM((8, 32, 1024), BF16),
            pltpu.VMEM((7, 32, 1024), BF16),
            pltpu.VMEM((32, 8, 128), F32),
            pltpu.VMEM((32, 8, 128), F32),
            dma((32,)), dma((32,)),
            dma((8, NSUB)), dma((8, NSUB)), dma((7, NSUB)), dma((7, NSUB)),
            dma((32,)), dma((32,)),
        ],
        compiler_params=pltpu.CompilerParams(
            collective_id=0, has_side_effects=True, vmem_limit_bytes=48 * 2**20
        ),
    )(rates, messages, spots, errors, focus)


def body(raw_pulses, range_weight, visibility, offsets, doppler_rate, phase_error, row_groups):
    first, twist, second, focus = dft_tables()
    z = lax.axis_index("tile") // 2
    signal = (raw_pulses * range_weight).reshape(2, 16, 128, 64).swapaxes(2, 3).reshape(2, 1024, 128)
    messages = compress(signal, jnp.asarray(first), jnp.asarray(twist), jnp.asarray(second))

    def plane(a):
        return lax.dynamic_slice_in_dim(a.reshape(32, 2, 2, 32, 4), z * 2, 2, 3)

    place = jnp.where(plane(visibility) != 0, plane(offsets), -8)
    place = place.transpose(0, 2, 4, 3, 1)
    same = jnp.eye(2, dtype=jnp.int32)[None, :, None, None, None, :, None]
    unit = jnp.arange(4, dtype=jnp.int32)[None, None, :, None, None, None, None]
    spots = jnp.where(same == 1, place[:, None, None] + unit, -8)
    spots = jnp.pad(spots.reshape(256, 32), ((0, 0), (0, 96))).astype(BF16)

    errors = lax.dynamic_slice_in_dim(phase_error, z * 2, 2, 0)
    labels = jnp.arange(16, dtype=jnp.int32)
    turn = jnp.sum(jnp.where(row_groups[None, :, None] == labels, errors[:, None, :], 0.0), axis=2)
    turn = jnp.repeat(turn, 4, axis=0)
    errors = jnp.stack([jnp.cos(turn), jnp.sin(turn)])
    focused = make_image(doppler_rate, messages, spots, errors, jnp.asarray(focus).astype(BF16))
    return focused[None]


def solution(mesh):
    return jax.shard_map(
        body,
        mesh=mesh,
        in_specs=(P(None, ("pulse", "tile", "row"), None), P(), P(), P(), P(), P(), P()),
        out_specs=P("tile", ("pulse", "row"), None),
        check_vma=False,
    )
```

```python
import math

import ml_dtypes
import numpy as np
import jax
import jax.numpy as jnp
from jax import lax
from jax.experimental import pallas as pl
from jax.experimental.pallas import tpu as pltpu
from jax.sharding import PartitionSpec as P

MESH = pl.DeviceIdType.MESH
F32 = jnp.float32
BF16 = jnp.bfloat16
TWO_PI = 2.0 * math.pi
PIECES = [(slice(r, r + 16), slice(c, c + 512)) for r in (0, 16) for c in (0, 512)]


def dft_tables():
    k, i = np.arange(64)[:, None], np.arange(64)[None, :]
    a = TWO_PI * (k * i % 64) / 64
    c, s = np.cos(a), np.sin(a)
    first = np.kron(np.block([[c, s], [-s, c]]), np.eye(8)).astype(ml_dtypes.bfloat16)
    bins = np.arange(128)[None, :]
    t = TWO_PI * (k * bins % 8192) / 8192
    twist = np.stack([np.cos(t), -np.sin(t)]).astype(np.float32)
    v = np.arange(128)[:, None]
    b = TWO_PI * (v * bins % 128) / 128
    c, s = np.cos(b), np.sin(b)
    order = np.concatenate([np.arange(0, 128, 2), np.arange(1, 128, 2)])
    second = np.concatenate([c[order], s[order]], axis=1).astype(ml_dtypes.bfloat16)
    focus = np.block([[c, s], [-s, c]]).astype(ml_dtypes.bfloat16)
    return first, twist, second, focus


def swap_bits(blocks, low):
    blocks = list(blocks)
    lane = lax.broadcasted_iota(jnp.int32, blocks[0].shape, 1)
    bit = 1
    while bit < len(blocks):
        shift = bit << low
        high = (lane & shift) != 0
        for i in range(len(blocks)):
            if i & bit == 0:
                a, b = blocks[i], blocks[i | bit]
                blocks[i] = jnp.where(high, pltpu.roll(b, shift, 1), a)
                blocks[i | bit] = jnp.where(high, b, pltpu.roll(a, 128 - shift, 1))
        bit *= 2
    return blocks


def unit_root(x):
    x = x - jnp.where(x >= 0.5, 1.0, 0.0)
    h = x * math.pi
    q = h * h
    sh = h * (1.0 + q * (-1 / 6 + q * (1 / 120 + q * (-1 / 5040 + q * (1 / 362880)))))
    ch = 1.0 + q * (-1 / 2 + q * (1 / 24 + q * (-1 / 720 + q * (1 / 40320 + q * (-1 / 3628800)))))
    return 1.0 - 2.0 * sh * sh, 2.0 * sh * ch


def distance(d):
    hops = [0, 1, 2, 1]
    return hops[(d >> 3) & 3] + hops[(d >> 1) & 3] + (d >> 5) + 0.3 * (d & 1)


PEERS = sorted(range(1, 64), key=lambda d: -distance(d))


def image_kernel(
    rate_ref, error_ref, raw_ref, taper_ref, offset_ref, seen_ref, group_ref,
    first_ref, twist_ref, second_ref, focus_ref, out_ref,
    signal, mid, terms, msg, recv, pick, gath, weight, phase, part_a, part_b,
    send_a, send_b, recv_a, recv_b, msg2, recv2,
    sem_s1, sem_r1, sem_sa, sem_ra, sem_sb, sem_rb, sem_s2, sem_r2,
):
    py = lax.axis_index("pulse")
    zc = lax.axis_index("tile")
    wx = lax.axis_index("row")
    core, zb, zp = zc & 1, (zc >> 1) & 1, zc >> 2

    def peer(d):
        p, w = (py + ((d >> 3) & 3)) & 3, (wx + ((d >> 1) & 3)) & 3
        b, c = zb ^ (d >> 5), core ^ (d & 1)
        return (p, zp * 4 + b * 2 + c, w), b * 32 + p * 8 + w * 2 + c, p * 8 + w * 2 + b

    me = zb * 32 + py * 8 + wx * 2 + core
    own_slot = (((py & 1) * 4 + wx) * 4 + zb * 2 + core) * 2 + (py >> 1)
    up = (py, (zc + 4) & 31, wx)
    down = (py, (zc + 28) & 31, wx)

    barrier = pltpu.get_barrier_semaphore()
    for d in PEERS:
        pl.semaphore_signal(barrier, inc=1, device_id=peer(d)[0], device_id_type=MESH)
    pl.semaphore_signal(barrier, inc=1, device_id=up, device_id_type=MESH)
    pl.semaphore_signal(barrier, inc=1, device_id=down, device_id_type=MESH)

    for ri in range(2):
        for i in range(0, 64, 2):
            halves = []
            for jh in range(2):
                pair = [
                    raw_ref[ri, jh * 8:jh * 8 + 8, n * 128:n * 128 + 128] * taper_ref[n:n + 1, :]
                    for n in (i, i + 1)
                ]
                halves.append(jnp.concatenate(pair, axis=0).astype(BF16))
            at = (ri * 64 + i) * 8
            signal[at:at + 16, 0:128] = halves[0]
            signal[at:at + 16, 128:256] = halves[1]
    mid[...] = jnp.dot(first_ref[...], signal[...], preferred_element_type=F32)

    def turn(k, carry):
        y_re = mid[pl.ds(pl.multiple_of(k * 8, 8), 8), :]
        y_im = mid[pl.ds(pl.multiple_of(512 + k * 8, 8), 8), :]
        t_re, t_im = twist_ref[0, pl.ds(k, 1), :], twist_ref[1, pl.ds(k, 1), :]
        res, ims = [], []
        for jh in range(2):
            a, b = y_re[:, jh * 128:jh * 128 + 128], y_im[:, jh * 128:jh * 128 + 128]
            res.append(a * t_re - b * t_im)
            ims.append(a * t_im + b * t_re)
        b_re, b_im = jnp.concatenate(res, axis=0), jnp.concatenate(ims, axis=0)
        at = pl.multiple_of(k * 32, 32)
        terms[pl.ds(at, 16), 0:128] = b_re.astype(BF16)
        terms[pl.ds(at, 16), 128:256] = b_im.astype(BF16)
        terms[pl.ds(at + 16, 16), 0:128] = b_im.astype(BF16)
        terms[pl.ds(at + 16, 16), 128:256] = (-b_re).astype(BF16)
        return carry

    lax.fori_loop(0, 64, turn, 0, unroll=4)

    def spectrum(n, carry):
        rows = terms[pl.ds(pl.multiple_of(n * 256, 256), 256), :]
        x = lax.dot_general(
            second_ref[...], rows, (((1,), (1,)), ((), ())), preferred_element_type=F32
        ) * (1.0 / math.sqrt(8192))
        for g in range(2):
            blocks = swap_bits([x[a * 32:a * 32 + 32, g * 128:g * 128 + 128] for a in range(4)], 5)
            for i in range(4):
                msg[n * 8 + g * 4 + i] = blocks[i].astype(BF16)
        return carry

    lax.fori_loop(0, 8, spectrum, 0)

    pl.semaphore_wait(barrier, 65)

    for d in PEERS:
        where, index, _ = peer(d)
        pltpu.make_async_remote_copy(
            src_ref=msg.at[index], dst_ref=recv.at[own_slot], send_sem=sem_s1.at[0], recv_sem=sem_r1.at[0],
            device_id=where, device_id_type=MESH,
        ).start()
    all_first = pltpu.make_async_remote_copy(
        src_ref=msg.at[pl.ds(0, 63)], dst_ref=recv.at[pl.ds(0, 63)], send_sem=sem_s1.at[0], recv_sem=sem_r1.at[0],
        device_id=peer(1)[0], device_id_type=MESH,
    )
    recv[own_slot] = msg[me]

    def azimuth(t, carry):
        rate = rate_ref[t]
        low = lax.broadcasted_iota(jnp.int32, (8, 512), 0)
        row = lax.broadcasted_iota(jnp.int32, (8, 512), 1)
        step = (low * rate) & 4095
        a_re, a_im = unit_root(((step * row) & 4095).astype(F32) * (1 / 4096))
        b_re, b_im = unit_root(((((step * 8) & 4095) * row) & 4095).astype(F32) * (1 / 4096))
        for w in range(4):
            parts_re, parts_im = [], []
            for k in (2 * w, 2 * w + 1):
                k_re, k_im = b_re[k:k + 1, :], b_im[k:k + 1, :]
                parts_re.append(a_re * k_re - a_im * k_im)
                parts_im.append(a_re * k_im + a_im * k_re)
            e_re = jnp.concatenate(parts_re, axis=0)
            e_im = jnp.concatenate(parts_im, axis=0)
            weight[t, w * 32:w * 32 + 16, 0:512] = e_re.astype(BF16)
            weight[t, w * 32:w * 32 + 16, 512:1024] = e_im.astype(BF16)
            weight[t, w * 32 + 16:w * 32 + 32, 0:512] = (-e_im).astype(BF16)
            weight[t, w * 32 + 16:w * 32 + 32, 512:1024] = e_re.astype(BF16)
        sub = lax.broadcasted_iota(jnp.int32, (16, 128), 0)
        lane = lax.broadcasted_iota(jnp.int32, (16, 128), 1)
        for p2 in range(2):
            sigma = p2 * 32 + zp * 4 + sub // 4
            s_re, s_im = unit_root(((((sigma * rate) & 63) * lane) & 63).astype(F32) * (1 / 64))
            phase[t, 2 * p2] = s_re
            phase[t, 2 * p2 + 1] = s_im
        return carry

    lax.fori_loop(0, 32, azimuth, 0)

    starts = jnp.where(seen_ref[...] != 0, offset_ref[...], -64).astype(F32).astype(BF16)
    sub = lax.broadcasted_iota(jnp.int32, (16, 256), 0)
    lane = lax.broadcasted_iota(jnp.int32, (16, 256), 1)
    unit = jnp.where((sub >> 2) == (lane >> 6), (lane & 31) - (sub & 3), 1000).astype(F32)

    def choose(n, carry):
        block = lax.broadcasted_iota(jnp.int32, (512, 256), 0)
        col = lax.broadcasted_iota(jnp.int32, (512, 256), 1)
        h, ss = (col >> 5) & 1, col >> 6
        here = (2 * h + (n >> 2)) * 128 + zp * 16 + ss * 4 + (n & 3)
        place = jnp.dot(starts, jnp.where(block == here, 1.0, 0.0).astype(BF16), preferred_element_type=F32)
        for t in range(32):
            line = place[t:t + 1, :]
            for uh in range(2):
                pick[n, uh, t * 16:t * 16 + 16, :] = jnp.where(line == unit + 32.0 * uh, 1.0, 0.0).astype(BF16)
        return carry

    lax.fori_loop(0, 8, choose, 0)

    all_first.wait_recv()

    def gather(n, carry):
        p2, part = n >> 2, n & 3
        rows = pl.ds(pl.multiple_of(part * 128, 128), 128)
        odd = (lax.broadcasted_iota(jnp.int32, (16, 128), 1) & 32) != 0
        found = []
        for w in range(4):
            data = recv[pl.ds(pl.multiple_of((p2 * 4 + w) * 8, 8), 8)].reshape(256, 128)
            found.append([
                jnp.dot(pick[p2 * 4 + w, uh, rows, :], data, preferred_element_type=F32) for uh in range(2)
            ])
        for i in range(8):
            m = [jnp.where(odd, f[1][i * 16:i * 16 + 16], f[0][i * 16:i * 16 + 16]) for f in found]
            pairs = [
                jnp.where(odd, m[k + 1] + pltpu.roll(m[k + 1], 32, 1), m[k] + pltpu.roll(m[k], 96, 1))
                for k in (0, 2)
            ]
            pairs = swap_bits(pairs, 6)
            for vi in range(2):
                gath[part * 8 + i, pl.ds(pl.multiple_of((vi * 2 + p2) * 16, 16), 16), :] = pairs[vi].astype(BF16)
        return carry

    lax.fori_loop(0, 8, gather, 0)

    def partial_image(dest, store):
        top = lax.broadcasted_iota(jnp.int32, (8, 128), 0) < 4
        for pair in range(2):
            sums = []
            for k in range(2):
                t = dest * 4 + pair * 2 + k
                y = jnp.dot(gath[t], weight[t], preferred_element_type=F32)
                s = [phase[t, i] for i in range(4)]
                mine = {}
                for g in range(4):
                    for vi in range(2):
                        tot_re = tot_im = None
                        for p2 in range(2):
                            rows = slice((vi * 2 + p2) * 16, (vi * 2 + p2) * 16 + 16)
                            y_re = y[rows, g * 128:g * 128 + 128]
                            y_im = y[rows, 512 + g * 128:640 + g * 128]
                            r = y_re * s[2 * p2] - y_im * s[2 * p2 + 1]
                            i = y_re * s[2 * p2 + 1] + y_im * s[2 * p2]
                            tot_re = r if tot_re is None else tot_re + r
                            tot_im = i if tot_im is None else tot_im + i
                        for ri, tot in ((0, tot_re), (1, tot_im)):
                            tot = tot[:8] + tot[8:]
                            mine[ri, g, vi] = tot + pltpu.roll(tot, 4, 0)
                sums.append(mine)
            for ri in range(2):
                for g in range(4):
                    for vi in range(2):
                        both = jnp.where(top, sums[0][ri, g, vi], sums[1][ri, g, vi])
                        row, at = vi * 16 + pair * 8, ri * 512 + g * 128
                        store[row:row + 8, at:at + 128] = both

    def ring_copy(src, dst, send_sem, recv_sem, step, h, where):
        rows, lanes = PIECES[h]
        return pltpu.make_async_remote_copy(
            src_ref=src.at[step, rows, lanes], dst_ref=dst.at[step, rows, lanes],
            send_sem=send_sem.at[step, h], recv_sem=recv_sem.at[step, h],
            device_id=where, device_id_type=MESH,
        )

    def copy_a(step, h):
        return ring_copy(send_a, recv_a, sem_sa, sem_ra, step, h, up)

    def copy_b(step, h):
        return ring_copy(send_b, recv_b, sem_sb, sem_rb, step, h, down)

    partial_image((zp + 4) & 7, part_a)
    for h in range(4):
        rows, lanes = PIECES[h]
        send, copy = (send_a, copy_a) if h < 2 else (send_b, copy_b)
        send[0, rows, lanes] = part_a[rows, lanes].astype(BF16)
        copy(0, h).start()
    for s in range(1, 4):
        partial_image((zp + 4 - s) & 7, part_a)
        partial_image((zp + 4 + s) & 7, part_b)
        for h in range(4):
            rows, lanes = PIECES[h]
            for part, send, got, copy, late in (
                (part_a, send_a, recv_a, copy_a, h < 2), (part_b, send_b, recv_b, copy_b, h >= 2)
            ):
                total = part[rows, lanes]
                if s > 1 or late:
                    copy(s - 1, h).wait_recv()
                    total = total + got[s - 1, rows, lanes].astype(F32)
                send[s, rows, lanes] = total.astype(BF16)
                copy(s, h).start()
    partial_image(zp, part_a)

    top = lax.broadcasted_iota(jnp.int32, (8, 128), 0) < 4
    turns = {}
    for q in range(4):
        labels = jnp.broadcast_to(group_ref[q:q + 1, :], (8, 128))
        for pair in range(2):
            angle = jnp.zeros((8, 128), F32)
            t = zp * 4 + pair * 2
            for n in range(16):
                angle = jnp.where(labels == n, jnp.where(top, error_ref[t, n], error_ref[t + 1, n]), angle)
            turns[q, pair] = unit_root(angle * (1.0 / TWO_PI))

    for h in range(4):
        rows, lanes = PIECES[h]
        copy_a(3, h).wait_recv()
        copy_b(3, h).wait_recv()
        part_a[rows, lanes] = (
            part_a[rows, lanes] + recv_a[3, rows, lanes].astype(F32) + recv_b[3, rows, lanes].astype(F32)
        )

    rights = []
    for vi in range(2):
        for q in range(4):
            for pair in range(2):
                row, at = vi * 16 + pair * 8, q * 128
                i_re = part_a[row:row + 8, at:at + 128]
                i_im = part_a[row:row + 8, 512 + at:640 + at]
                c, s = turns[q, pair]
                rights.append(jnp.concatenate([i_re * c - i_im * s, i_re * s + i_im * c], axis=1))
    right = (jnp.concatenate(rights, axis=0) * (1.0 / 1024)).astype(BF16)
    spun = lax.dot_general(focus_ref[...], right, (((1,), (1,)), ((), ())), preferred_element_type=F32)
    for w in range(4):
        blocks = []
        for i in range(8):
            at = (i // 4) * 128 + w * 32 + (i % 4) * 8
            blocks.append(spun[at:at + 8, :])
        blocks = swap_bits(blocks, 3)
        for i in range(8):
            msg2[(i // 2) * 8 + w * 2 + i % 2] = blocks[i]

    for d in PEERS:
        where, _, index = peer(d)
        pltpu.make_async_remote_copy(
            src_ref=msg2.at[index], dst_ref=recv2.at[me], send_sem=sem_s2.at[0], recv_sem=sem_r2.at[0],
            device_id=where, device_id_type=MESH,
        ).start()
    recv2[me] = msg2[py * 8 + wx * 2 + zb]

    all_first.wait_send()
    for s in range(4):
        for h in range(4):
            if s > 0 or h < 2:
                copy_a(s, h).wait_send()
            if s > 0 or h >= 2:
                copy_b(s, h).wait_send()
    all_last = pltpu.make_async_remote_copy(
        src_ref=recv2.at[pl.ds(0, 63)], dst_ref=recv2.at[pl.ds(0, 63)], send_sem=sem_s2.at[0], recv_sem=sem_r2.at[0],
        device_id=peer(1)[0], device_id_type=MESH,
    )
    all_last.wait_recv()

    high = (lax.broadcasted_iota(jnp.int32, (8, 128), 1) & 4) != 0
    blocks = []
    for n in range(32):
        k = (n >> 2) * 8 + (n & 3)
        a, b = recv2[k], recv2[k + 4]
        even = jnp.where(high, pltpu.roll(b, 4, 1), a)
        odd = jnp.where(high, b, pltpu.roll(a, 124, 1))
        blocks.append(jnp.where(core == 0, even, odd))
    low = swap_bits_of(blocks, ((1, 1), (2, 2), (4, 8), (8, 16), (16, 32)))
    for i in range(32):
        ri, hi, unit_at = i // 16, (i // 4) % 4, i % 4
        at = ri * 512 + unit_at * 128
        out_ref[hi * 8:hi * 8 + 8, at:at + 128] = low[i]
    all_last.wait_send()


def swap_bits_of(blocks, pairs):
    blocks = list(blocks)
    lane = lax.broadcasted_iota(jnp.int32, blocks[0].shape, 1)
    for bit, shift in pairs:
        high = (lane & shift) != 0
        for i in range(len(blocks)):
            if i & bit == 0:
                a, b = blocks[i], blocks[i | bit]
                blocks[i] = jnp.where(high, pltpu.roll(b, shift, 1), a)
                blocks[i | bit] = jnp.where(high, b, pltpu.roll(a, 128 - shift, 1))
    return blocks


def body(raw_pulses, range_weight, visibility, offsets, doppler_rate, phase_error, row_groups):
    first, twist, second, focus = dft_tables()
    vmem = pl.BlockSpec(memory_space=pltpu.VMEM)
    smem = pl.BlockSpec(memory_space=pltpu.SMEM)
    dma = pltpu.SemaphoreType.DMA
    focused = pl.pallas_call(
        image_kernel,
        out_shape=jax.ShapeDtypeStruct((32, 1024), F32),
        in_specs=[smem, smem] + [vmem] * 9,
        out_specs=vmem,
        scratch_shapes=[
            pltpu.VMEM((1024, 256), BF16),
            pltpu.VMEM((1024, 256), F32),
            pltpu.VMEM((2048, 256), BF16),
            pltpu.VMEM((64, 32, 128), BF16),
            pltpu.VMEM((64, 32, 128), BF16),
            pltpu.VMEM((8, 2, 512, 256), BF16),
            pltpu.VMEM((32, 64, 128), BF16),
            pltpu.VMEM((32, 128, 1024), BF16),
            pltpu.VMEM((32, 4, 16, 128), F32),
            pltpu.VMEM((32, 1024), F32),
            pltpu.VMEM((32, 1024), F32),
            pltpu.VMEM((4, 32, 1024), BF16),
            pltpu.VMEM((4, 32, 1024), BF16),
            pltpu.VMEM((4, 32, 1024), BF16),
            pltpu.VMEM((4, 32, 1024), BF16),
            pltpu.VMEM((32, 8, 128), F32),
            pltpu.VMEM((64, 8, 128), F32),
            dma((1,)), dma((1,)),
            dma((4, 4)), dma((4, 4)), dma((4, 4)), dma((4, 4)),
            dma((1,)), dma((1,)),
        ],
        compiler_params=pltpu.CompilerParams(
            collective_id=0, has_side_effects=True, vmem_limit_bytes=48 * 2**20
        ),
    )(
        doppler_rate, phase_error, raw_pulses, range_weight.reshape(64, 128), offsets, visibility,
        row_groups.reshape(4, 128), jnp.asarray(first), jnp.asarray(twist), jnp.asarray(second), jnp.asarray(focus),
    )
    return focused[None]


def solution(mesh):
    return jax.shard_map(
        body,
        mesh=mesh,
        in_specs=(P(None, ("pulse", "tile", "row"), None), P(), P(), P(), P(), P(), P()),
        out_specs=P("tile", ("pulse", "row"), None),
        check_vma=False,
    )
```

```python
import math

import ml_dtypes
import numpy as np
import jax
import jax.numpy as jnp
from jax import lax
from jax.experimental import pallas as pl
from jax.experimental.pallas import tpu as pltpu
from jax.sharding import PartitionSpec as P

MESH = pl.DeviceIdType.MESH
F32 = jnp.float32
BF16 = jnp.bfloat16
TWO_PI = 2.0 * math.pi
PIECES = [(slice(r, r + 16), slice(c, c + 512)) for r in (0, 16) for c in (0, 512)]


def dft_tables():
    k, i = np.arange(64)[:, None], np.arange(64)[None, :]
    a = TWO_PI * (k * i % 64) / 64
    c, s = np.cos(a), np.sin(a)
    first = np.kron(np.block([[c, s], [-s, c]]), np.eye(8)).astype(ml_dtypes.bfloat16)
    bins = np.arange(128)[None, :]
    t = TWO_PI * (k * bins % 8192) / 8192
    twist = np.stack([np.cos(t), -np.sin(t)]).astype(np.float32)
    v = np.arange(128)[:, None]
    b = TWO_PI * (v * bins % 128) / 128
    c, s = np.cos(b), np.sin(b)
    order = np.concatenate([np.arange(0, 128, 2), np.arange(1, 128, 2)])
    second = np.concatenate([c[order], s[order]], axis=1).astype(ml_dtypes.bfloat16)
    focus = np.block([[c, s], [-s, c]]).astype(ml_dtypes.bfloat16)
    return first, twist, second, focus


def swap_bits(blocks, low):
    blocks = list(blocks)
    lane = lax.broadcasted_iota(jnp.int32, blocks[0].shape, 1)
    bit = 1
    while bit < len(blocks):
        shift = bit << low
        high = (lane & shift) != 0
        for i in range(len(blocks)):
            if i & bit == 0:
                a, b = blocks[i], blocks[i | bit]
                blocks[i] = jnp.where(high, pltpu.roll(b, shift, 1), a)
                blocks[i | bit] = jnp.where(high, b, pltpu.roll(a, 128 - shift, 1))
        bit *= 2
    return blocks


def unit_root(x):
    x = x - jnp.where(x >= 0.5, 1.0, 0.0)
    h = x * math.pi
    q = h * h
    sh = h * (1.0 + q * (-1 / 6 + q * (1 / 120 + q * (-1 / 5040 + q * (1 / 362880)))))
    ch = 1.0 + q * (-1 / 2 + q * (1 / 24 + q * (-1 / 720 + q * (1 / 40320 + q * (-1 / 3628800)))))
    return 1.0 - 2.0 * sh * sh, 2.0 * sh * ch


def distance(d):
    hops = [0, 1, 2, 1]
    return hops[(d >> 3) & 3] + hops[(d >> 1) & 3] + (d >> 5) + 0.3 * (d & 1)


PEERS = sorted(range(1, 64), key=lambda d: -distance(d))
PEERS_BY_PARITY = [d for d in PEERS if (d >> 3) & 1 == 0] + [d for d in PEERS if (d >> 3) & 1 == 1]


def image_kernel(
    rate_in, error_in, raw_in, taper_in, offset_in, seen_in, group_in,
    first_in, twist_in, second_in, focus_in, out_ref,
    rate_ref, error_ref, raw_ref, taper_ref, offset_ref, seen_ref, group_ref,
    first_ref, twist_ref, second_ref, focus_ref, sem_in,
    signal, mid, terms, msg, recv, pick, gath, weight, phase, part_a, part_b,
    send_a, send_b, recv_a, recv_b, msg2, recv2,
    sem_s1, sem_r1, sem_sa, sem_ra, sem_sb, sem_rb, sem_s2, sem_r2,
):
    py = lax.axis_index("pulse")
    zc = lax.axis_index("tile")
    wx = lax.axis_index("row")
    core, zb, zp = zc & 1, (zc >> 1) & 1, zc >> 2

    def peer(d):
        p, w = (py + ((d >> 3) & 3)) & 3, (wx + ((d >> 1) & 3)) & 3
        b, c = zb ^ (d >> 5), core ^ (d & 1)
        return (p, zp * 4 + b * 2 + c, w), b * 32 + p * 8 + w * 2 + c, p * 8 + w * 2 + b

    me = zb * 32 + py * 8 + wx * 2 + core
    own_slot = (((py & 1) * 4 + wx) * 4 + zb * 2 + core) * 2 + (py >> 1)
    up = (py, (zc + 4) & 31, wx)
    down = (py, (zc + 28) & 31, wx)

    loads = [
        pltpu.make_async_copy(a, b, sem_in.at[i])
        for i, (a, b) in enumerate((
            (raw_in, raw_ref), (first_in, first_ref), (taper_in, taper_ref), (twist_in, twist_ref),
            (second_in, second_ref), (rate_in, rate_ref), (offset_in, offset_ref), (seen_in, seen_ref),
            (error_in, error_ref), (group_in, group_ref), (focus_in, focus_ref),
        ))
    ]
    for load in loads:
        load.start()

    barrier = pltpu.get_barrier_semaphore()
    for d in PEERS:
        pl.semaphore_signal(barrier, inc=1, device_id=peer(d)[0], device_id_type=MESH)
    pl.semaphore_signal(barrier, inc=1, device_id=up, device_id_type=MESH)
    pl.semaphore_signal(barrier, inc=1, device_id=down, device_id_type=MESH)

    for i in (0, 2):
        loads[i].wait()
    for ri in range(2):
        for i in range(0, 64, 2):
            halves = []
            for jh in range(2):
                pair = [
                    raw_ref[ri, jh * 8:jh * 8 + 8, n * 128:n * 128 + 128] * taper_ref[n:n + 1, :]
                    for n in (i, i + 1)
                ]
                halves.append(jnp.concatenate(pair, axis=0).astype(BF16))
            at = (ri * 64 + i) * 8
            signal[at:at + 16, 0:128] = halves[0]
            signal[at:at + 16, 128:256] = halves[1]
    loads[1].wait()
    mid[...] = jnp.dot(first_ref[...], signal[...], preferred_element_type=F32)

    for i in (3, 4):
        loads[i].wait()

    def turn(k, carry):
        y_re = mid[pl.ds(pl.multiple_of(k * 8, 8), 8), :]
        y_im = mid[pl.ds(pl.multiple_of(512 + k * 8, 8), 8), :]
        t_re, t_im = twist_ref[0, pl.ds(k, 1), :], twist_ref[1, pl.ds(k, 1), :]
        res, ims = [], []
        for jh in range(2):
            a, b = y_re[:, jh * 128:jh * 128 + 128], y_im[:, jh * 128:jh * 128 + 128]
            res.append(a * t_re - b * t_im)
            ims.append(a * t_im + b * t_re)
        b_re, b_im = jnp.concatenate(res, axis=0), jnp.concatenate(ims, axis=0)
        at = pl.multiple_of(k * 32, 32)
        terms[pl.ds(at, 16), 0:128] = b_re.astype(BF16)
        terms[pl.ds(at, 16), 128:256] = b_im.astype(BF16)
        terms[pl.ds(at + 16, 16), 0:128] = b_im.astype(BF16)
        terms[pl.ds(at + 16, 16), 128:256] = (-b_re).astype(BF16)
        return carry

    lax.fori_loop(0, 64, turn, 0, unroll=4)

    def spectrum(n, carry):
        rows = terms[pl.ds(pl.multiple_of(n * 256, 256), 256), :]
        x = lax.dot_general(
            second_ref[...], rows, (((1,), (1,)), ((), ())), preferred_element_type=F32
        ) * (1.0 / math.sqrt(8192))
        for g in range(2):
            blocks = swap_bits([x[a * 32:a * 32 + 32, g * 128:g * 128 + 128] for a in range(4)], 5)
            for i in range(4):
                msg[n * 8 + g * 4 + i] = blocks[i].astype(BF16)
        return carry

    lax.fori_loop(0, 8, spectrum, 0)

    pl.semaphore_wait(barrier, 65)

    parity = py & 1
    for d in PEERS_BY_PARITY:
        where, index, _ = peer(d)
        pltpu.make_async_remote_copy(
            src_ref=msg.at[index], dst_ref=recv.at[own_slot], send_sem=sem_s1.at[0], recv_sem=sem_r1.at[parity],
            device_id=where, device_id_type=MESH,
        ).start()
    all_first = pltpu.make_async_remote_copy(
        src_ref=msg.at[pl.ds(0, 63)], dst_ref=recv.at[pl.ds(0, 63)], send_sem=sem_s1.at[0], recv_sem=sem_r1.at[0],
        device_id=peer(1)[0], device_id_type=MESH,
    )
    pltpu.make_async_copy(msg.at[me], recv.at[own_slot], sem_r1.at[parity]).start()

    def half_first(p2):
        half = pl.ds(pl.multiple_of(p2 * 32, 32), 32)
        return pltpu.make_async_remote_copy(
            src_ref=msg.at[pl.ds(0, 32)], dst_ref=recv.at[half], send_sem=sem_s1.at[0], recv_sem=sem_r1.at[p2],
            device_id=peer(1)[0], device_id_type=MESH,
        )

    for load in loads[5:]:
        load.wait()

    def azimuth(t, carry):
        rate = rate_ref[t]
        low = lax.broadcasted_iota(jnp.int32, (8, 512), 0)
        row = lax.broadcasted_iota(jnp.int32, (8, 512), 1)
        step = (low * rate) & 4095
        a_re, a_im = unit_root(((step * row) & 4095).astype(F32) * (1 / 4096))
        b_re, b_im = unit_root(((((step * 8) & 4095) * row) & 4095).astype(F32) * (1 / 4096))
        for w in range(4):
            parts_re, parts_im = [], []
            for k in (2 * w, 2 * w + 1):
                k_re, k_im = b_re[k:k + 1, :], b_im[k:k + 1, :]
                parts_re.append(a_re * k_re - a_im * k_im)
                parts_im.append(a_re * k_im + a_im * k_re)
            e_re = jnp.concatenate(parts_re, axis=0)
            e_im = jnp.concatenate(parts_im, axis=0)
            weight[t, w * 32:w * 32 + 16, 0:512] = e_re.astype(BF16)
            weight[t, w * 32:w * 32 + 16, 512:1024] = e_im.astype(BF16)
            weight[t, w * 32 + 16:w * 32 + 32, 0:512] = (-e_im).astype(BF16)
            weight[t, w * 32 + 16:w * 32 + 32, 512:1024] = e_re.astype(BF16)
        sub = lax.broadcasted_iota(jnp.int32, (16, 128), 0)
        lane = lax.broadcasted_iota(jnp.int32, (16, 128), 1)
        for p2 in range(2):
            sigma = p2 * 32 + zp * 4 + sub // 4
            s_re, s_im = unit_root(((((sigma * rate) & 63) * lane) & 63).astype(F32) * (1 / 64))
            phase[t, 2 * p2] = s_re
            phase[t, 2 * p2 + 1] = s_im
        return carry

    lax.fori_loop(0, 32, azimuth, 0)

    starts = jnp.where(seen_ref[...] != 0, offset_ref[...], -64).astype(F32).astype(BF16)
    sub = lax.broadcasted_iota(jnp.int32, (16, 256), 0)
    lane = lax.broadcasted_iota(jnp.int32, (16, 256), 1)
    unit = jnp.where((sub >> 2) == (lane >> 6), (lane & 31) - (sub & 3), 1000).astype(F32)

    def choose(n, carry):
        block = lax.broadcasted_iota(jnp.int32, (512, 256), 0)
        col = lax.broadcasted_iota(jnp.int32, (512, 256), 1)
        h, ss = (col >> 5) & 1, col >> 6
        here = (2 * h + (n >> 2)) * 128 + zp * 16 + ss * 4 + (n & 3)
        place = jnp.dot(starts, jnp.where(block == here, 1.0, 0.0).astype(BF16), preferred_element_type=F32)
        for t in range(32):
            line = place[t:t + 1, :]
            for uh in range(2):
                pick[n, uh, t * 16:t * 16 + 16, :] = jnp.where(line == unit + 32.0 * uh, 1.0, 0.0).astype(BF16)
        return carry

    lax.fori_loop(0, 8, choose, 0)

    def gather(p2, part):
        rows = pl.ds(pl.multiple_of(part * 128, 128), 128)
        odd = (lax.broadcasted_iota(jnp.int32, (16, 128), 1) & 32) != 0
        found = []
        for w in range(4):
            data = recv[pl.ds(pl.multiple_of((p2 * 4 + w) * 8, 8), 8)].reshape(256, 128)
            found.append([
                jnp.dot(pick[p2 * 4 + w, uh, rows, :], data, preferred_element_type=F32) for uh in range(2)
            ])
        for i in range(8):
            m = [jnp.where(odd, f[1][i * 16:i * 16 + 16], f[0][i * 16:i * 16 + 16]) for f in found]
            pairs = [
                jnp.where(odd, m[k + 1] + pltpu.roll(m[k + 1], 32, 1), m[k] + pltpu.roll(m[k], 96, 1))
                for k in (0, 2)
            ]
            pairs = swap_bits(pairs, 6)
            for vi in range(2):
                gath[part * 8 + i, pl.ds(pl.multiple_of((vi * 2 + p2) * 16, 16), 16), :] = pairs[vi].astype(BF16)

    def gather_early(part, carry):
        gather(parity, part)
        return carry

    def gather_late(part, carry):
        gather(1 - parity, (far + part) & 3)
        return carry

    far = ((zp + 4) & 7) >> 1
    half_first(parity).wait_recv()
    lax.fori_loop(0, 4, gather_early, 0)
    half_first(1 - parity).wait_recv()
    gather(1 - parity, far)

    def partial_image(dest, store):
        top = lax.broadcasted_iota(jnp.int32, (8, 128), 0) < 4
        for pair in range(2):
            sums = []
            for k in range(2):
                t = dest * 4 + pair * 2 + k
                y = jnp.dot(gath[t], weight[t], preferred_element_type=F32)
                s = [phase[t, i] for i in range(4)]
                mine = {}
                for g in range(4):
                    for vi in range(2):
                        tot_re = tot_im = None
                        for p2 in range(2):
                            rows = slice((vi * 2 + p2) * 16, (vi * 2 + p2) * 16 + 16)
                            y_re = y[rows, g * 128:g * 128 + 128]
                            y_im = y[rows, 512 + g * 128:640 + g * 128]
                            r = y_re * s[2 * p2] - y_im * s[2 * p2 + 1]
                            i = y_re * s[2 * p2 + 1] + y_im * s[2 * p2]
                            tot_re = r if tot_re is None else tot_re + r
                            tot_im = i if tot_im is None else tot_im + i
                        for ri, tot in ((0, tot_re), (1, tot_im)):
                            tot = tot[:8] + tot[8:]
                            mine[ri, g, vi] = tot + pltpu.roll(tot, 4, 0)
                sums.append(mine)
            for ri in range(2):
                for g in range(4):
                    for vi in range(2):
                        both = jnp.where(top, sums[0][ri, g, vi], sums[1][ri, g, vi])
                        row, at = vi * 16 + pair * 8, ri * 512 + g * 128
                        store[row:row + 8, at:at + 128] = both

    def ring_copy(src, dst, send_sem, recv_sem, step, h, where):
        rows, lanes = PIECES[h]
        return pltpu.make_async_remote_copy(
            src_ref=src.at[step, rows, lanes], dst_ref=dst.at[step, rows, lanes],
            send_sem=send_sem.at[step, h], recv_sem=recv_sem.at[step, h],
            device_id=where, device_id_type=MESH,
        )

    def copy_a(step, h):
        return ring_copy(send_a, recv_a, sem_sa, sem_ra, step, h, up)

    def copy_b(step, h):
        return ring_copy(send_b, recv_b, sem_sb, sem_rb, step, h, down)

    partial_image((zp + 4) & 7, part_a)
    for h in range(4):
        rows, lanes = PIECES[h]
        send, copy = (send_a, copy_a) if h < 2 else (send_b, copy_b)
        send[0, rows, lanes] = part_a[rows, lanes].astype(BF16)
        copy(0, h).start()
    lax.fori_loop(1, 4, gather_late, 0)
    for s in range(1, 4):
        partial_image((zp + 4 - s) & 7, part_a)
        partial_image((zp + 4 + s) & 7, part_b)
        for h in range(4):
            rows, lanes = PIECES[h]
            for part, send, got, copy, late in (
                (part_a, send_a, recv_a, copy_a, h < 2), (part_b, send_b, recv_b, copy_b, h >= 2)
            ):
                total = part[rows, lanes]
                if s > 1 or late:
                    copy(s - 1, h).wait_recv()
                    total = total + got[s - 1, rows, lanes].astype(F32)
                send[s, rows, lanes] = total.astype(BF16)
                copy(s, h).start()
    partial_image(zp, part_a)

    top = lax.broadcasted_iota(jnp.int32, (8, 128), 0) < 4
    turns = {}
    for q in range(4):
        labels = jnp.broadcast_to(group_ref[q:q + 1, :], (8, 128))
        for pair in range(2):
            angle = jnp.zeros((8, 128), F32)
            t = zp * 4 + pair * 2
            for n in range(16):
                angle = jnp.where(labels == n, jnp.where(top, error_ref[n, t], error_ref[n, t + 1]), angle)
            turns[q, pair] = unit_root(angle * (1.0 / TWO_PI))

    for h in range(4):
        rows, lanes = PIECES[h]
        copy_a(3, h).wait_recv()
        copy_b(3, h).wait_recv()
        part_a[rows, lanes] = (
            part_a[rows, lanes] + recv_a[3, rows, lanes].astype(F32) + recv_b[3, rows, lanes].astype(F32)
        )

    rights = []
    for vi in range(2):
        for q in range(4):
            for pair in range(2):
                row, at = vi * 16 + pair * 8, q * 128
                i_re = part_a[row:row + 8, at:at + 128]
                i_im = part_a[row:row + 8, 512 + at:640 + at]
                c, s = turns[q, pair]
                rights.append(jnp.concatenate([i_re * c - i_im * s, i_re * s + i_im * c], axis=1))
    right = (jnp.concatenate(rights, axis=0) * (1.0 / 1024)).astype(BF16)
    spun = lax.dot_general(focus_ref[...], right, (((1,), (1,)), ((), ())), preferred_element_type=F32)
    for w in range(4):
        blocks = []
        for i in range(8):
            at = (i // 4) * 128 + w * 32 + (i % 4) * 8
            blocks.append(spun[at:at + 8, :])
        blocks = swap_bits(blocks, 3)
        for i in range(8):
            msg2[(i // 2) * 8 + w * 2 + i % 2] = blocks[i]

    for d in PEERS:
        where, _, index = peer(d)
        pltpu.make_async_remote_copy(
            src_ref=msg2.at[index], dst_ref=recv2.at[me], send_sem=sem_s2.at[0], recv_sem=sem_r2.at[0],
            device_id=where, device_id_type=MESH,
        ).start()
    recv2[me] = msg2[py * 8 + wx * 2 + zb]

    all_first.wait_send()
    for s in range(4):
        for h in range(4):
            if s > 0 or h < 2:
                copy_a(s, h).wait_send()
            if s > 0 or h >= 2:
                copy_b(s, h).wait_send()
    all_last = pltpu.make_async_remote_copy(
        src_ref=recv2.at[pl.ds(0, 63)], dst_ref=recv2.at[pl.ds(0, 63)], send_sem=sem_s2.at[0], recv_sem=sem_r2.at[0],
        device_id=peer(1)[0], device_id_type=MESH,
    )
    all_last.wait_recv()

    high = (lax.broadcasted_iota(jnp.int32, (8, 128), 1) & 4) != 0
    blocks = []
    for n in range(32):
        k = (n >> 2) * 8 + (n & 3)
        a, b = recv2[k], recv2[k + 4]
        even = jnp.where(high, pltpu.roll(b, 4, 1), a)
        odd = jnp.where(high, b, pltpu.roll(a, 124, 1))
        blocks.append(jnp.where(core == 0, even, odd))
    low = swap_bits_of(blocks, ((1, 1), (2, 2), (4, 8), (8, 16), (16, 32)))
    for i in range(32):
        ri, hi, unit_at = i // 16, (i // 4) % 4, i % 4
        at = ri * 512 + unit_at * 128
        out_ref[hi * 8:hi * 8 + 8, at:at + 128] = low[i]
    all_last.wait_send()


def swap_bits_of(blocks, pairs):
    blocks = list(blocks)
    lane = lax.broadcasted_iota(jnp.int32, blocks[0].shape, 1)
    for bit, shift in pairs:
        high = (lane & shift) != 0
        for i in range(len(blocks)):
            if i & bit == 0:
                a, b = blocks[i], blocks[i | bit]
                blocks[i] = jnp.where(high, pltpu.roll(b, shift, 1), a)
                blocks[i | bit] = jnp.where(high, b, pltpu.roll(a, 128 - shift, 1))
    return blocks


def body(raw_pulses, range_weight, visibility, offsets, doppler_rate, phase_error, row_groups):
    first, twist, second, focus = dft_tables()
    vmem = pl.BlockSpec(memory_space=pltpu.VMEM)
    hbm = pl.BlockSpec(memory_space=pltpu.HBM)
    dma = pltpu.SemaphoreType.DMA
    focused = pl.pallas_call(
        image_kernel,
        out_shape=jax.ShapeDtypeStruct((32, 1024), F32),
        in_specs=[hbm] * 11,
        out_specs=vmem,
        scratch_shapes=[
            pltpu.SMEM((32,), jnp.int32),
            pltpu.SMEM((16, 32), F32),
            pltpu.VMEM((2, 16, 8192), F32),
            pltpu.VMEM((64, 128), F32),
            pltpu.VMEM((32, 512), jnp.int32),
            pltpu.VMEM((32, 512), jnp.int32),
            pltpu.VMEM((4, 128), jnp.int32),
            pltpu.VMEM((1024, 1024), BF16),
            pltpu.VMEM((2, 64, 128), F32),
            pltpu.VMEM((128, 256), BF16),
            pltpu.VMEM((256, 256), BF16),
            dma((11,)),
            pltpu.VMEM((1024, 256), BF16),
            pltpu.VMEM((1024, 256), F32),
            pltpu.VMEM((2048, 256), BF16),
            pltpu.VMEM((64, 32, 128), BF16),
            pltpu.VMEM((64, 32, 128), BF16),
            pltpu.VMEM((8, 2, 512, 256), BF16),
            pltpu.VMEM((32, 64, 128), BF16),
            pltpu.VMEM((32, 128, 1024), BF16),
            pltpu.VMEM((32, 4, 16, 128), F32),
            pltpu.VMEM((32, 1024), F32),
            pltpu.VMEM((32, 1024), F32),
            pltpu.VMEM((4, 32, 1024), BF16),
            pltpu.VMEM((4, 32, 1024), BF16),
            pltpu.VMEM((4, 32, 1024), BF16),
            pltpu.VMEM((4, 32, 1024), BF16),
            pltpu.VMEM((32, 8, 128), F32),
            pltpu.VMEM((64, 8, 128), F32),
            dma((1,)), dma((2,)),
            dma((4, 4)), dma((4, 4)), dma((4, 4)), dma((4, 4)),
            dma((1,)), dma((1,)),
        ],
        compiler_params=pltpu.CompilerParams(
            collective_id=0, has_side_effects=True, vmem_limit_bytes=62 * 2**20
        ),
    )(
        doppler_rate, phase_error.T, raw_pulses, range_weight.reshape(64, 128), offsets, visibility,
        row_groups.reshape(4, 128), jnp.asarray(first), jnp.asarray(twist), jnp.asarray(second), jnp.asarray(focus),
    )
    return focused[None]


def solution(mesh):
    return jax.shard_map(
        body,
        mesh=mesh,
        in_specs=(P(None, ("pulse", "tile", "row"), None), P(), P(), P(), P(), P(), P()),
        out_specs=P("tile", ("pulse", "row"), None),
        check_vma=False,
    )
```

```python
import math

import ml_dtypes
import numpy as np
import jax
import jax.numpy as jnp
from jax import lax
from jax.experimental import pallas as pl
from jax.experimental.pallas import tpu as pltpu
from jax.sharding import PartitionSpec as P

MESH = pl.DeviceIdType.MESH
F32 = jnp.float32
BF16 = jnp.bfloat16
TWO_PI = 2.0 * math.pi
PIECES = [(slice(r, r + 16), slice(c, c + 512)) for r in (0, 16) for c in (0, 512)]


def dft_tables():
    k, i = np.arange(64)[:, None], np.arange(64)[None, :]
    a = TWO_PI * (k * i % 64) / 64
    c, s = np.cos(a), np.sin(a)
    first = np.kron(np.block([[c, s], [-s, c]]), np.eye(8)).astype(ml_dtypes.bfloat16)
    bins = np.arange(128)[None, :]
    t = TWO_PI * (k * bins % 8192) / 8192
    twist = np.stack([np.cos(t), -np.sin(t)]).astype(np.float32)
    v = np.arange(128)[:, None]
    b = TWO_PI * (v * bins % 128) / 128
    c, s = np.cos(b), np.sin(b)
    order = np.concatenate([np.arange(0, 128, 2), np.arange(1, 128, 2)])
    second = np.concatenate([c[order], s[order]], axis=1).astype(ml_dtypes.bfloat16)
    focus = np.block([[c, s], [-s, c]]).astype(ml_dtypes.bfloat16)
    return first, twist, second, focus


def swap_bits(blocks, low):
    blocks = list(blocks)
    lane = lax.broadcasted_iota(jnp.int32, blocks[0].shape, 1)
    bit = 1
    while bit < len(blocks):
        shift = bit << low
        high = (lane & shift) != 0
        for i in range(len(blocks)):
            if i & bit == 0:
                a, b = blocks[i], blocks[i | bit]
                blocks[i] = jnp.where(high, pltpu.roll(b, shift, 1), a)
                blocks[i | bit] = jnp.where(high, b, pltpu.roll(a, 128 - shift, 1))
        bit *= 2
    return blocks


def unit_root(x):
    x = x - jnp.where(x >= 0.5, 1.0, 0.0)
    h = x * math.pi
    q = h * h
    sh = h * (1.0 + q * (-1 / 6 + q * (1 / 120 + q * (-1 / 5040 + q * (1 / 362880)))))
    ch = 1.0 + q * (-1 / 2 + q * (1 / 24 + q * (-1 / 720 + q * (1 / 40320 + q * (-1 / 3628800)))))
    return 1.0 - 2.0 * sh * sh, 2.0 * sh * ch


def distance(d):
    hops = [0, 1, 2, 1]
    return hops[(d >> 3) & 3] + hops[(d >> 1) & 3] + (d >> 5) + 0.3 * (d & 1)


PEERS = sorted(range(1, 64), key=lambda d: -distance(d))
PEERS_BY_PARITY = [d for d in PEERS if (d >> 3) & 1 == 0] + [d for d in PEERS if (d >> 3) & 1 == 1]


def image_kernel(
    rate_in, error_in, raw_in, taper_in, offset_in, seen_in, group_in,
    first_in, twist_in, second_in, focus_in, out_ref,
    rate_ref, error_ref, raw_ref, taper_ref, offset_ref, seen_ref, group_ref,
    first_ref, twist_ref, second_ref, focus_ref, sem_in,
    signal, mid, terms, msg, recv, pick, gath, weight, phase, part_a, part_b,
    send_a, send_b, recv_a, recv_b, send_f, recv_f, msg2, recv2,
    sem_s1, sem_r1, sem_sa, sem_ra, sem_sb, sem_rb, sem_sf, sem_rf, sem_s2, sem_r2,
):
    py = lax.axis_index("pulse")
    zc = lax.axis_index("tile")
    wx = lax.axis_index("row")
    core, zb, zp = zc & 1, (zc >> 1) & 1, zc >> 2

    def peer(d):
        p, w = (py + ((d >> 3) & 3)) & 3, (wx + ((d >> 1) & 3)) & 3
        b, c = zb ^ (d >> 5), core ^ (d & 1)
        return (p, zp * 4 + b * 2 + c, w), b * 32 + p * 8 + w * 2 + c, p * 8 + w * 2 + b

    me = zb * 32 + py * 8 + wx * 2 + core
    own_slot = (((py & 1) * 4 + wx) * 4 + zb * 2 + core) * 2 + (py >> 1)
    up = (py, (zc + 4) & 31, wx)
    down = (py, (zc + 28) & 31, wx)
    up2 = (py, (zc + 8) & 31, wx)
    down2 = (py, (zc + 24) & 31, wx)

    loads = [
        pltpu.make_async_copy(a, b, sem_in.at[i])
        for i, (a, b) in enumerate((
            (raw_in, raw_ref), (first_in, first_ref), (taper_in, taper_ref), (twist_in, twist_ref),
            (second_in, second_ref), (rate_in, rate_ref), (offset_in, offset_ref), (seen_in, seen_ref),
            (error_in, error_ref), (group_in, group_ref), (focus_in, focus_ref),
        ))
    ]
    for load in loads:
        load.start()

    barrier = pltpu.get_barrier_semaphore()
    for d in PEERS:
        pl.semaphore_signal(barrier, inc=1, device_id=peer(d)[0], device_id_type=MESH)
    for where in (up2, down2, up, down):
        pl.semaphore_signal(barrier, inc=1, device_id=where, device_id_type=MESH)

    for i in (0, 2):
        loads[i].wait()
    for ri in range(2):
        for i in range(0, 64, 2):
            halves = []
            for jh in range(2):
                pair = [
                    raw_ref[ri, jh * 8:jh * 8 + 8, n * 128:n * 128 + 128] * taper_ref[n:n + 1, :]
                    for n in (i, i + 1)
                ]
                halves.append(jnp.concatenate(pair, axis=0).astype(BF16))
            at = (ri * 64 + i) * 8
            signal[at:at + 16, 0:128] = halves[0]
            signal[at:at + 16, 128:256] = halves[1]
    loads[1].wait()
    mid[...] = jnp.dot(first_ref[...], signal[...], preferred_element_type=F32)

    for i in (3, 4):
        loads[i].wait()

    def turn(k, carry):
        y_re = mid[pl.ds(pl.multiple_of(k * 8, 8), 8), :]
        y_im = mid[pl.ds(pl.multiple_of(512 + k * 8, 8), 8), :]
        t_re, t_im = twist_ref[0, pl.ds(k, 1), :], twist_ref[1, pl.ds(k, 1), :]
        res, ims = [], []
        for jh in range(2):
            a, b = y_re[:, jh * 128:jh * 128 + 128], y_im[:, jh * 128:jh * 128 + 128]
            res.append(a * t_re - b * t_im)
            ims.append(a * t_im + b * t_re)
        b_re, b_im = jnp.concatenate(res, axis=0), jnp.concatenate(ims, axis=0)
        at = pl.multiple_of(k * 32, 32)
        terms[pl.ds(at, 16), 0:128] = b_re.astype(BF16)
        terms[pl.ds(at, 16), 128:256] = b_im.astype(BF16)
        terms[pl.ds(at + 16, 16), 0:128] = b_im.astype(BF16)
        terms[pl.ds(at + 16, 16), 128:256] = (-b_re).astype(BF16)
        return carry

    lax.fori_loop(0, 64, turn, 0, unroll=8)

    for n in range(8):
        rows = terms[n * 256:n * 256 + 256, :]
        x = lax.dot_general(
            second_ref[...], rows, (((1,), (1,)), ((), ())), preferred_element_type=F32
        ) * (1.0 / math.sqrt(8192))
        for g in range(2):
            blocks = swap_bits([x[a * 32:a * 32 + 32, g * 128:g * 128 + 128] for a in range(4)], 5)
            for i in range(4):
                msg[n * 8 + g * 4 + i] = blocks[i].astype(BF16)

    pl.semaphore_wait(barrier, 67)

    parity = py & 1
    for d in PEERS_BY_PARITY:
        where, index, _ = peer(d)
        pltpu.make_async_remote_copy(
            src_ref=msg.at[index], dst_ref=recv.at[own_slot], send_sem=sem_s1.at[0], recv_sem=sem_r1.at[parity],
            device_id=where, device_id_type=MESH,
        ).start()
    all_first = pltpu.make_async_remote_copy(
        src_ref=msg.at[pl.ds(0, 63)], dst_ref=recv.at[pl.ds(0, 63)], send_sem=sem_s1.at[0], recv_sem=sem_r1.at[0],
        device_id=peer(1)[0], device_id_type=MESH,
    )
    pltpu.make_async_copy(msg.at[me], recv.at[own_slot], sem_r1.at[parity]).start()

    def half_first(p2):
        half = pl.ds(pl.multiple_of(p2 * 32, 32), 32)
        return pltpu.make_async_remote_copy(
            src_ref=msg.at[pl.ds(0, 32)], dst_ref=recv.at[half], send_sem=sem_s1.at[0], recv_sem=sem_r1.at[p2],
            device_id=peer(1)[0], device_id_type=MESH,
        )

    for load in loads[5:]:
        load.wait()

    def azimuth(t, carry):
        rate = rate_ref[t]
        low = lax.broadcasted_iota(jnp.int32, (8, 512), 0)
        row = lax.broadcasted_iota(jnp.int32, (8, 512), 1)
        step = (low * rate) & 4095
        a_re, a_im = unit_root(((step * row) & 4095).astype(F32) * (1 / 4096))
        b_re, b_im = unit_root(((((step * 8) & 4095) * row) & 4095).astype(F32) * (1 / 4096))
        for w in range(4):
            parts_re, parts_im = [], []
            for k in (2 * w, 2 * w + 1):
                k_re, k_im = b_re[k:k + 1, :], b_im[k:k + 1, :]
                parts_re.append(a_re * k_re - a_im * k_im)
                parts_im.append(a_re * k_im + a_im * k_re)
            e_re = jnp.concatenate(parts_re, axis=0)
            e_im = jnp.concatenate(parts_im, axis=0)
            weight[t, w * 32:w * 32 + 16, 0:512] = e_re.astype(BF16)
            weight[t, w * 32:w * 32 + 16, 512:1024] = e_im.astype(BF16)
            weight[t, w * 32 + 16:w * 32 + 32, 0:512] = (-e_im).astype(BF16)
            weight[t, w * 32 + 16:w * 32 + 32, 512:1024] = e_re.astype(BF16)
        sub = lax.broadcasted_iota(jnp.int32, (16, 128), 0)
        lane = lax.broadcasted_iota(jnp.int32, (16, 128), 1)
        for p2 in range(2):
            sigma = p2 * 32 + zp * 4 + sub // 4
            s_re, s_im = unit_root(((((sigma * rate) & 63) * lane) & 63).astype(F32) * (1 / 64))
            phase[t, 2 * p2] = s_re
            phase[t, 2 * p2 + 1] = s_im
        return carry

    lax.fori_loop(0, 32, azimuth, 0)

    starts = jnp.where(seen_ref[...] != 0, offset_ref[...], -64).astype(F32).astype(BF16)
    sub = lax.broadcasted_iota(jnp.int32, (16, 256), 0)
    lane = lax.broadcasted_iota(jnp.int32, (16, 256), 1)
    unit = jnp.where((sub >> 2) == (lane >> 6), (lane & 31) - (sub & 3), 1000).astype(F32)

    def choose(n, carry):
        block = lax.broadcasted_iota(jnp.int32, (512, 256), 0)
        col = lax.broadcasted_iota(jnp.int32, (512, 256), 1)
        h, ss = (col >> 5) & 1, col >> 6
        here = (2 * h + (n >> 2)) * 128 + zp * 16 + ss * 4 + (n & 3)
        place = jnp.dot(starts, jnp.where(block == here, 1.0, 0.0).astype(BF16), preferred_element_type=F32)
        for t in range(32):
            line = place[t:t + 1, :]
            for uh in range(2):
                pick[n, uh, t * 16:t * 16 + 16, :] = jnp.where(line == unit + 32.0 * uh, 1.0, 0.0).astype(BF16)
        return carry

    lax.fori_loop(0, 8, choose, 0)

    def gather(p2, part):
        rows = pl.ds(pl.multiple_of(part * 128, 128), 128)
        odd = (lax.broadcasted_iota(jnp.int32, (16, 128), 1) & 32) != 0
        found = []
        for w in range(4):
            data = recv[pl.ds(pl.multiple_of((p2 * 4 + w) * 8, 8), 8)].reshape(256, 128)
            found.append([
                jnp.dot(pick[p2 * 4 + w, uh, rows, :], data, preferred_element_type=F32) for uh in range(2)
            ])
        for i in range(8):
            m = [jnp.where(odd, f[1][i * 16:i * 16 + 16], f[0][i * 16:i * 16 + 16]) for f in found]
            pairs = [
                jnp.where(odd, m[k + 1] + pltpu.roll(m[k + 1], 32, 1), m[k] + pltpu.roll(m[k], 96, 1))
                for k in (0, 2)
            ]
            pairs = swap_bits(pairs, 6)
            for vi in range(2):
                gath[part * 8 + i, pl.ds(pl.multiple_of((vi * 2 + p2) * 16, 16), 16), :] = pairs[vi].astype(BF16)

    def gather_early(part, carry):
        gather(parity, part)
        return carry

    far = ((zp + 4) & 7) >> 1
    side = jnp.where((zp & 1) == 1, 1, 3)
    half_first(parity).wait_recv()
    lax.fori_loop(0, 4, gather_early, 0)
    half_first(1 - parity).wait_recv()
    gather(1 - parity, far)

    def partial_image(dest, store):
        top = lax.broadcasted_iota(jnp.int32, (8, 128), 0) < 4
        for pair in range(2):
            sums = []
            for k in range(2):
                t = dest * 4 + pair * 2 + k
                y = jnp.dot(gath[t], weight[t], preferred_element_type=F32)
                s = [phase[t, i] for i in range(4)]
                mine = {}
                for g in range(4):
                    for vi in range(2):
                        tot_re = tot_im = None
                        for p2 in range(2):
                            rows = slice((vi * 2 + p2) * 16, (vi * 2 + p2) * 16 + 16)
                            y_re = y[rows, g * 128:g * 128 + 128]
                            y_im = y[rows, 512 + g * 128:640 + g * 128]
                            r = y_re * s[2 * p2] - y_im * s[2 * p2 + 1]
                            i = y_re * s[2 * p2 + 1] + y_im * s[2 * p2]
                            tot_re = r if tot_re is None else tot_re + r
                            tot_im = i if tot_im is None else tot_im + i
                        for ri, tot in ((0, tot_re), (1, tot_im)):
                            tot = tot[:8] + tot[8:]
                            mine[ri, g, vi] = tot + pltpu.roll(tot, 4, 0)
                sums.append(mine)
            for ri in range(2):
                for g in range(4):
                    for vi in range(2):
                        both = jnp.where(top, sums[0][ri, g, vi], sums[1][ri, g, vi])
                        row, at = vi * 16 + pair * 8, ri * 512 + g * 128
                        store[row:row + 8, at:at + 128] = both

    def ring_copy(src, dst, send_sem, recv_sem, step, h, where):
        rows, lanes = PIECES[h]
        return pltpu.make_async_remote_copy(
            src_ref=src.at[step, rows, lanes], dst_ref=dst.at[step, rows, lanes],
            send_sem=send_sem.at[step, h], recv_sem=recv_sem.at[step, h],
            device_id=where, device_id_type=MESH,
        )

    def copy_a(step, h):
        return ring_copy(send_a, recv_a, sem_sa, sem_ra, step, h, up)

    def copy_b(step, h):
        return ring_copy(send_b, recv_b, sem_sb, sem_rb, step, h, down)

    def copy_far(k, h):
        rows, lanes = PIECES[h]
        return pltpu.make_async_remote_copy(
            src_ref=send_f.at[rows, lanes], dst_ref=recv_f.at[rows, lanes],
            send_sem=sem_sf.at[h], recv_sem=sem_rf.at[h],
            device_id=(up2, down2)[k], device_id_type=MESH,
        )

    partial_image((zp + 4) & 7, part_a)
    for h in range(4):
        rows, lanes = PIECES[h]
        send_f[rows, lanes] = part_a[rows, lanes].astype(BF16)
        copy_far(h // 2, h).start()
    gather(1 - parity, (far + side) & 3)
    for s in range(3):
        partial_image((zp + 3 - s) & 7, part_a)
        partial_image((zp + 5 + s) & 7, part_b)
        for h in range(4):
            rows, lanes = PIECES[h]
            for k, (part, send, got, copy) in enumerate(
                ((part_a, send_a, recv_a, copy_a), (part_b, send_b, recv_b, copy_b))
            ):
                total = part[rows, lanes]
                if s > 0:
                    if s == 1 and h // 2 == k:
                        copy_far(k, h).wait_recv()
                        total = total + recv_f[rows, lanes].astype(F32)
                    copy(s - 1, h).wait_recv()
                    total = total + got[s - 1, rows, lanes].astype(F32)
                send[s, rows, lanes] = total.astype(BF16)
                copy(s, h).start()
        if s == 0:
            gather(1 - parity, (far + 2) & 3)
            gather(1 - parity, (far - side) & 3)
    partial_image(zp, part_a)

    top = lax.broadcasted_iota(jnp.int32, (8, 128), 0) < 4
    turns = {}
    for q in range(4):
        labels = jnp.broadcast_to(group_ref[q:q + 1, :], (8, 128))
        for pair in range(2):
            angle = jnp.zeros((8, 128), F32)
            t = zp * 4 + pair * 2
            for n in range(16):
                angle = jnp.where(labels == n, jnp.where(top, error_ref[n, t], error_ref[n, t + 1]), angle)
            turns[q, pair] = unit_root(angle * (1.0 / TWO_PI))

    for h in range(4):
        rows, lanes = PIECES[h]
        copy_a(2, h).wait_recv()
        copy_b(2, h).wait_recv()
        part_a[rows, lanes] = (
            part_a[rows, lanes] + recv_a[2, rows, lanes].astype(F32) + recv_b[2, rows, lanes].astype(F32)
        )

    rights = []
    for vi in range(2):
        for q in range(4):
            for pair in range(2):
                row, at = vi * 16 + pair * 8, q * 128
                i_re = part_a[row:row + 8, at:at + 128]
                i_im = part_a[row:row + 8, 512 + at:640 + at]
                c, s = turns[q, pair]
                rights.append(jnp.concatenate([i_re * c - i_im * s, i_re * s + i_im * c], axis=1))
    right = (jnp.concatenate(rights, axis=0) * (1.0 / 1024)).astype(BF16)
    mid[0:256, 0:128] = lax.dot_general(
        focus_ref[...], right, (((1,), (1,)), ((), ())), preferred_element_type=F32
    )
    for dw in (2, 1, 3, 0):
        w = (wx + dw) & 3
        blocks = []
        for i in range(8):
            at = pl.multiple_of((i // 4) * 128 + w * 32 + (i % 4) * 8, 8)
            blocks.append(mid[pl.ds(at, 8), 0:128])
        blocks = swap_bits(blocks, 3)
        for i in range(8):
            msg2[(i // 2) * 8 + w * 2 + i % 2] = blocks[i]
        for d in PEERS:
            if (d >> 1) & 3 == dw:
                where, _, index = peer(d)
                pltpu.make_async_remote_copy(
                    src_ref=msg2.at[index], dst_ref=recv2.at[me], send_sem=sem_s2.at[0], recv_sem=sem_r2.at[0],
                    device_id=where, device_id_type=MESH,
                ).start()
    recv2[me] = msg2[py * 8 + wx * 2 + zb]

    all_first.wait_send()
    for h in range(4):
        copy_far(h // 2, h).wait_send()
        for s in range(3):
            copy_a(s, h).wait_send()
            copy_b(s, h).wait_send()
    all_last = pltpu.make_async_remote_copy(
        src_ref=recv2.at[pl.ds(0, 63)], dst_ref=recv2.at[pl.ds(0, 63)], send_sem=sem_s2.at[0], recv_sem=sem_r2.at[0],
        device_id=peer(1)[0], device_id_type=MESH,
    )
    all_last.wait_recv()

    high = (lax.broadcasted_iota(jnp.int32, (8, 128), 1) & 4) != 0
    blocks = []
    for n in range(32):
        k = (n >> 2) * 8 + (n & 3)
        a, b = recv2[k], recv2[k + 4]
        even = jnp.where(high, pltpu.roll(b, 4, 1), a)
        odd = jnp.where(high, b, pltpu.roll(a, 124, 1))
        blocks.append(jnp.where(core == 0, even, odd))
    low = swap_bits_of(blocks, ((1, 1), (2, 2), (4, 8), (8, 16), (16, 32)))
    for i in range(32):
        ri, hi, unit_at = i // 16, (i // 4) % 4, i % 4
        at = ri * 512 + unit_at * 128
        out_ref[hi * 8:hi * 8 + 8, at:at + 128] = low[i]
    all_last.wait_send()


def swap_bits_of(blocks, pairs):
    blocks = list(blocks)
    lane = lax.broadcasted_iota(jnp.int32, blocks[0].shape, 1)
    for bit, shift in pairs:
        high = (lane & shift) != 0
        for i in range(len(blocks)):
            if i & bit == 0:
                a, b = blocks[i], blocks[i | bit]
                blocks[i] = jnp.where(high, pltpu.roll(b, shift, 1), a)
                blocks[i | bit] = jnp.where(high, b, pltpu.roll(a, 128 - shift, 1))
    return blocks


def body(raw_pulses, range_weight, visibility, offsets, doppler_rate, phase_error, row_groups):
    first, twist, second, focus = dft_tables()
    vmem = pl.BlockSpec(memory_space=pltpu.VMEM)
    hbm = pl.BlockSpec(memory_space=pltpu.HBM)
    dma = pltpu.SemaphoreType.DMA
    focused = pl.pallas_call(
        image_kernel,
        out_shape=jax.ShapeDtypeStruct((32, 1024), F32),
        in_specs=[hbm] * 11,
        out_specs=vmem,
        scratch_shapes=[
            pltpu.SMEM((32,), jnp.int32),
            pltpu.SMEM((16, 32), F32),
            pltpu.VMEM((2, 16, 8192), F32),
            pltpu.VMEM((64, 128), F32),
            pltpu.VMEM((32, 512), jnp.int32),
            pltpu.VMEM((32, 512), jnp.int32),
            pltpu.VMEM((4, 128), jnp.int32),
            pltpu.VMEM((1024, 1024), BF16),
            pltpu.VMEM((2, 64, 128), F32),
            pltpu.VMEM((128, 256), BF16),
            pltpu.VMEM((256, 256), BF16),
            dma((11,)),
            pltpu.VMEM((1024, 256), BF16),
            pltpu.VMEM((1024, 256), F32),
            pltpu.VMEM((2048, 256), BF16),
            pltpu.VMEM((64, 32, 128), BF16),
            pltpu.VMEM((64, 32, 128), BF16),
            pltpu.VMEM((8, 2, 512, 256), BF16),
            pltpu.VMEM((32, 64, 128), BF16),
            pltpu.VMEM((32, 128, 1024), BF16),
            pltpu.VMEM((32, 4, 16, 128), F32),
            pltpu.VMEM((32, 1024), F32),
            pltpu.VMEM((32, 1024), F32),
            pltpu.VMEM((3, 32, 1024), BF16),
            pltpu.VMEM((3, 32, 1024), BF16),
            pltpu.VMEM((3, 32, 1024), BF16),
            pltpu.VMEM((3, 32, 1024), BF16),
            pltpu.VMEM((32, 1024), BF16),
            pltpu.VMEM((32, 1024), BF16),
            pltpu.VMEM((32, 8, 128), F32),
            pltpu.VMEM((64, 8, 128), F32),
            dma((1,)), dma((2,)),
            dma((3, 4)), dma((3, 4)), dma((3, 4)), dma((3, 4)),
            dma((4,)), dma((4,)),
            dma((1,)), dma((1,)),
        ],
        compiler_params=pltpu.CompilerParams(
            collective_id=0, has_side_effects=True, vmem_limit_bytes=62 * 2**20
        ),
    )(
        doppler_rate, phase_error.T, raw_pulses, range_weight.reshape(64, 128), offsets, visibility,
        row_groups.reshape(4, 128), jnp.asarray(first), jnp.asarray(twist), jnp.asarray(second), jnp.asarray(focus),
    )
    return focused[None]


def solution(mesh):
    return jax.shard_map(
        body,
        mesh=mesh,
        in_specs=(P(None, ("pulse", "tile", "row"), None), P(), P(), P(), P(), P(), P()),
        out_specs=P("tile", ("pulse", "row"), None),
        check_vma=False,
    )
```

```python
import math

import ml_dtypes
import numpy as np
import jax
import jax.numpy as jnp
from jax import lax
from jax.experimental import pallas as pl
from jax.experimental.pallas import tpu as pltpu
from jax.sharding import PartitionSpec as P

MESH = pl.DeviceIdType.MESH
F32 = jnp.float32
BF16 = jnp.bfloat16
TWO_PI = 2.0 * math.pi
PIECES = [(slice(r, r + 16), slice(c, c + 512)) for r in (0, 16) for c in (0, 512)]


def dft_tables():
    k, i = np.arange(64)[:, None], np.arange(64)[None, :]
    a = TWO_PI * (k * i % 64) / 64
    c, s = np.cos(a), np.sin(a)
    first = np.kron(np.block([[c, s], [-s, c]]), np.eye(8)).astype(ml_dtypes.bfloat16)
    bins = np.arange(128)[None, :]
    t = TWO_PI * (k * bins % 8192) / 8192
    twist = np.stack([np.cos(t), -np.sin(t)]).astype(np.float32)
    v = np.arange(128)[:, None]
    b = TWO_PI * (v * bins % 128) / 128
    c, s = np.cos(b), np.sin(b)
    order = np.concatenate([np.arange(0, 128, 2), np.arange(1, 128, 2)])
    second = np.concatenate([c[order], s[order]], axis=1).astype(ml_dtypes.bfloat16)
    focus = np.block([[c, s], [-s, c]]).astype(ml_dtypes.bfloat16)
    return first, twist, second, focus


def swap_bits(blocks, low):
    blocks = list(blocks)
    lane = lax.broadcasted_iota(jnp.int32, blocks[0].shape, 1)
    bit = 1
    while bit < len(blocks):
        shift = bit << low
        high = (lane & shift) != 0
        for i in range(len(blocks)):
            if i & bit == 0:
                a, b = blocks[i], blocks[i | bit]
                blocks[i] = jnp.where(high, pltpu.roll(b, shift, 1), a)
                blocks[i | bit] = jnp.where(high, b, pltpu.roll(a, 128 - shift, 1))
        bit *= 2
    return blocks


def unit_root(x):
    x = x - jnp.where(x >= 0.5, 1.0, 0.0)
    h = x * math.pi
    q = h * h
    sh = h * (1.0 + q * (-1 / 6 + q * (1 / 120 + q * (-1 / 5040 + q * (1 / 362880)))))
    ch = 1.0 + q * (-1 / 2 + q * (1 / 24 + q * (-1 / 720 + q * (1 / 40320 + q * (-1 / 3628800)))))
    return 1.0 - 2.0 * sh * sh, 2.0 * sh * ch


def distance(d):
    hops = [0, 1, 2, 1]
    return hops[(d >> 3) & 3] + hops[(d >> 1) & 3] + (d >> 5) + 0.3 * (d & 1)


PEERS = sorted(range(1, 64), key=lambda d: -distance(d))
PEERS_BY_PARITY = [d for d in PEERS if (d >> 3) & 1 == 0] + [d for d in PEERS if (d >> 3) & 1 == 1]


def image_kernel(
    rate_in, error_in, raw_in, taper_in, offset_in, seen_in, group_in,
    first_in, twist_in, second_in, focus_in, out_ref,
    rate_ref, error_ref, raw_ref, taper_ref, offset_ref, seen_ref, group_ref,
    first_ref, twist_ref, second_ref, focus_ref, sem_in,
    signal, mid, terms, msg, recv, pick, gath, weight, phase, part_a, part_b,
    send_a, send_b, recv_a, recv_b, send_f, recv_f, msg2, recv2,
    sem_s1, sem_r1, sem_sa, sem_ra, sem_sb, sem_rb, sem_sf, sem_rf, sem_s2, sem_r2,
):
    py = lax.axis_index("pulse")
    zc = lax.axis_index("tile")
    wx = lax.axis_index("row")
    core, zb, zp = zc & 1, (zc >> 1) & 1, zc >> 2

    def peer(d):
        p, w = (py + ((d >> 3) & 3)) & 3, (wx + ((d >> 1) & 3)) & 3
        b, c = zb ^ (d >> 5), core ^ (d & 1)
        return (p, zp * 4 + b * 2 + c, w), b * 32 + p * 8 + w * 2 + c, p * 8 + w * 2 + b

    me = zb * 32 + py * 8 + wx * 2 + core
    own_slot = (((py & 1) * 4 + wx) * 4 + zb * 2 + core) * 2 + (py >> 1)
    up = (py, (zc + 4) & 31, wx)
    down = (py, (zc + 28) & 31, wx)
    up2 = (py, (zc + 8) & 31, wx)
    down2 = (py, (zc + 24) & 31, wx)

    loads = [
        pltpu.make_async_copy(a, b, sem_in.at[i])
        for i, (a, b) in enumerate((
            (raw_in, raw_ref), (first_in, first_ref), (taper_in, taper_ref), (twist_in, twist_ref),
            (second_in, second_ref), (rate_in, rate_ref), (offset_in, offset_ref), (seen_in, seen_ref),
            (error_in, error_ref), (group_in, group_ref), (focus_in, focus_ref),
        ))
    ]
    for load in loads:
        load.start()

    barrier = pltpu.get_barrier_semaphore()
    for d in PEERS:
        pl.semaphore_signal(barrier, inc=1, device_id=peer(d)[0], device_id_type=MESH)
    for where in (up2, down2, up, down):
        pl.semaphore_signal(barrier, inc=1, device_id=where, device_id_type=MESH)

    for i in (0, 2):
        loads[i].wait()
    for ri in range(2):
        for i in range(0, 64, 2):
            halves = []
            for jh in range(2):
                pair = [
                    raw_ref[ri, jh * 8:jh * 8 + 8, n * 128:n * 128 + 128] * taper_ref[n:n + 1, :]
                    for n in (i, i + 1)
                ]
                halves.append(jnp.concatenate(pair, axis=0).astype(BF16))
            at = (ri * 64 + i) * 8
            signal[at:at + 16, 0:128] = halves[0]
            signal[at:at + 16, 128:256] = halves[1]
    loads[1].wait()
    mid[...] = jnp.dot(first_ref[...], signal[...], preferred_element_type=F32)

    for i in (3, 4):
        loads[i].wait()

    def turn(k, carry):
        y_re = mid[pl.ds(pl.multiple_of(k * 8, 8), 8), :]
        y_im = mid[pl.ds(pl.multiple_of(512 + k * 8, 8), 8), :]
        t_re, t_im = twist_ref[0, pl.ds(k, 1), :], twist_ref[1, pl.ds(k, 1), :]
        res, ims = [], []
        for jh in range(2):
            a, b = y_re[:, jh * 128:jh * 128 + 128], y_im[:, jh * 128:jh * 128 + 128]
            res.append(a * t_re - b * t_im)
            ims.append(a * t_im + b * t_re)
        b_re, b_im = jnp.concatenate(res, axis=0), jnp.concatenate(ims, axis=0)
        at = pl.multiple_of(k * 32, 32)
        terms[pl.ds(at, 16), 0:128] = b_re.astype(BF16)
        terms[pl.ds(at, 16), 128:256] = b_im.astype(BF16)
        terms[pl.ds(at + 16, 16), 0:128] = b_im.astype(BF16)
        terms[pl.ds(at + 16, 16), 128:256] = (-b_re).astype(BF16)
        return carry

    lax.fori_loop(0, 64, turn, 0, unroll=8)

    for n in range(8):
        rows = terms[n * 256:n * 256 + 256, :]
        x = lax.dot_general(
            second_ref[...], rows, (((1,), (1,)), ((), ())), preferred_element_type=F32
        ) * (1.0 / math.sqrt(8192))
        for g in range(2):
            blocks = swap_bits([x[a * 32:a * 32 + 32, g * 128:g * 128 + 128] for a in range(4)], 5)
            for i in range(4):
                msg[n * 8 + g * 4 + i] = blocks[i].astype(BF16)

    pl.semaphore_wait(barrier, 67)

    parity = py & 1
    for d in PEERS_BY_PARITY:
        where, index, _ = peer(d)
        pltpu.make_async_remote_copy(
            src_ref=msg.at[index], dst_ref=recv.at[own_slot], send_sem=sem_s1.at[0], recv_sem=sem_r1.at[parity],
            device_id=where, device_id_type=MESH,
        ).start()
    all_first = pltpu.make_async_remote_copy(
        src_ref=msg.at[pl.ds(0, 63)], dst_ref=recv.at[pl.ds(0, 63)], send_sem=sem_s1.at[0], recv_sem=sem_r1.at[0],
        device_id=peer(1)[0], device_id_type=MESH,
    )
    pltpu.make_async_copy(msg.at[me], recv.at[own_slot], sem_r1.at[parity]).start()

    def half_first(p2):
        half = pl.ds(pl.multiple_of(p2 * 32, 32), 32)
        return pltpu.make_async_remote_copy(
            src_ref=msg.at[pl.ds(0, 32)], dst_ref=recv.at[half], send_sem=sem_s1.at[0], recv_sem=sem_r1.at[p2],
            device_id=peer(1)[0], device_id_type=MESH,
        )

    for load in loads[5:]:
        load.wait()

    def azimuth(t, carry):
        rate = rate_ref[t]
        low = lax.broadcasted_iota(jnp.int32, (8, 512), 0)
        row = lax.broadcasted_iota(jnp.int32, (8, 512), 1)
        step = (low * rate) & 4095
        a_re, a_im = unit_root(((step * row) & 4095).astype(F32) * (1 / 4096))
        b_re, b_im = unit_root(((((step * 8) & 4095) * row) & 4095).astype(F32) * (1 / 4096))
        for w in range(4):
            parts_re, parts_im = [], []
            for k in (2 * w, 2 * w + 1):
                k_re, k_im = b_re[k:k + 1, :], b_im[k:k + 1, :]
                parts_re.append(a_re * k_re - a_im * k_im)
                parts_im.append(a_re * k_im + a_im * k_re)
            e_re = jnp.concatenate(parts_re, axis=0)
            e_im = jnp.concatenate(parts_im, axis=0)
            weight[t, w * 32:w * 32 + 16, 0:512] = e_re.astype(BF16)
            weight[t, w * 32:w * 32 + 16, 512:1024] = e_im.astype(BF16)
            weight[t, w * 32 + 16:w * 32 + 32, 0:512] = (-e_im).astype(BF16)
            weight[t, w * 32 + 16:w * 32 + 32, 512:1024] = e_re.astype(BF16)
        sub = lax.broadcasted_iota(jnp.int32, (16, 128), 0)
        lane = lax.broadcasted_iota(jnp.int32, (16, 128), 1)
        for p2 in range(2):
            sigma = p2 * 32 + zp * 4 + sub // 4
            s_re, s_im = unit_root(((((sigma * rate) & 63) * lane) & 63).astype(F32) * (1 / 64))
            phase[t, 2 * p2] = s_re
            phase[t, 2 * p2 + 1] = s_im
        return carry

    lax.fori_loop(0, 32, azimuth, 0)

    starts = jnp.where(seen_ref[...] != 0, offset_ref[...], -64).astype(F32).astype(BF16)
    sub = lax.broadcasted_iota(jnp.int32, (16, 256), 0)
    lane = lax.broadcasted_iota(jnp.int32, (16, 256), 1)
    unit = jnp.where((sub >> 2) == (lane >> 6), (lane & 31) - (sub & 3), 1000).astype(F32)

    def choose(n, carry):
        block = lax.broadcasted_iota(jnp.int32, (512, 256), 0)
        col = lax.broadcasted_iota(jnp.int32, (512, 256), 1)
        h, ss = (col >> 5) & 1, col >> 6
        here = (2 * h + (n >> 2)) * 128 + zp * 16 + ss * 4 + (n & 3)
        place = jnp.dot(starts, jnp.where(block == here, 1.0, 0.0).astype(BF16), preferred_element_type=F32)
        for t in range(32):
            line = place[t:t + 1, :]
            for uh in range(2):
                pick[n, uh, t * 16:t * 16 + 16, :] = jnp.where(line == unit + 32.0 * uh, 1.0, 0.0).astype(BF16)
        return carry

    lax.fori_loop(0, 8, choose, 0)

    def gather(p2, part):
        rows = pl.ds(pl.multiple_of(part * 128, 128), 128)
        odd = (lax.broadcasted_iota(jnp.int32, (16, 128), 1) & 32) != 0
        found = []
        for w in range(4):
            data = recv[pl.ds(pl.multiple_of((p2 * 4 + w) * 8, 8), 8)].reshape(256, 128)
            found.append([
                jnp.dot(pick[p2 * 4 + w, uh, rows, :], data, preferred_element_type=F32) for uh in range(2)
            ])
        for i in range(8):
            m = [jnp.where(odd, f[1][i * 16:i * 16 + 16], f[0][i * 16:i * 16 + 16]) for f in found]
            pairs = [
                jnp.where(odd, m[k + 1] + pltpu.roll(m[k + 1], 32, 1), m[k] + pltpu.roll(m[k], 96, 1))
                for k in (0, 2)
            ]
            pairs = swap_bits(pairs, 6)
            for vi in range(2):
                gath[part * 8 + i, pl.ds(pl.multiple_of((vi * 2 + p2) * 16, 16), 16), :] = pairs[vi].astype(BF16)

    def gather_early(part, carry):
        gather(parity, part)
        return carry

    far = ((zp + 4) & 7) >> 1
    side = jnp.where((zp & 1) == 1, 1, 3)
    half_first(parity).wait_recv()
    lax.fori_loop(0, 4, gather_early, 0)
    half_first(1 - parity).wait_recv()
    gather(1 - parity, far)

    def partial_image(dest, store):
        top = lax.broadcasted_iota(jnp.int32, (8, 128), 0) < 4
        for pair in range(2):
            sums = []
            for k in range(2):
                t = dest * 4 + pair * 2 + k
                y = jnp.dot(gath[t], weight[t], preferred_element_type=F32)
                s = [phase[t, i] for i in range(4)]
                mine = {}
                for g in range(4):
                    for vi in range(2):
                        tot_re = tot_im = None
                        for p2 in range(2):
                            rows = slice((vi * 2 + p2) * 16, (vi * 2 + p2) * 16 + 16)
                            y_re = y[rows, g * 128:g * 128 + 128]
                            y_im = y[rows, 512 + g * 128:640 + g * 128]
                            r = y_re * s[2 * p2] - y_im * s[2 * p2 + 1]
                            i = y_re * s[2 * p2 + 1] + y_im * s[2 * p2]
                            tot_re = r if tot_re is None else tot_re + r
                            tot_im = i if tot_im is None else tot_im + i
                        for ri, tot in ((0, tot_re), (1, tot_im)):
                            tot = tot[:8] + tot[8:]
                            mine[ri, g, vi] = tot + pltpu.roll(tot, 4, 0)
                sums.append(mine)
            for ri in range(2):
                for g in range(4):
                    for vi in range(2):
                        both = jnp.where(top, sums[0][ri, g, vi], sums[1][ri, g, vi])
                        row, at = vi * 16 + pair * 8, ri * 512 + g * 128
                        store[row:row + 8, at:at + 128] = both

    def ring_copy(src, dst, send_sem, recv_sem, step, h, where):
        rows, lanes = PIECES[h]
        return pltpu.make_async_remote_copy(
            src_ref=src.at[step, rows, lanes], dst_ref=dst.at[step, rows, lanes],
            send_sem=send_sem.at[step, h], recv_sem=recv_sem.at[step, h],
            device_id=where, device_id_type=MESH,
        )

    def copy_a(step, h):
        return ring_copy(send_a, recv_a, sem_sa, sem_ra, step, h, up)

    def copy_b(step, h):
        return ring_copy(send_b, recv_b, sem_sb, sem_rb, step, h, down)

    def copy_far(k, h):
        rows, lanes = PIECES[h]
        return pltpu.make_async_remote_copy(
            src_ref=send_f.at[rows, lanes], dst_ref=recv_f.at[rows, lanes],
            send_sem=sem_sf.at[h], recv_sem=sem_rf.at[h],
            device_id=(up2, down2)[k], device_id_type=MESH,
        )

    partial_image((zp + 4) & 7, part_a)
    for h in range(4):
        rows, lanes = PIECES[h]
        send_f[rows, lanes] = part_a[rows, lanes].astype(BF16)
        copy_far(h // 2, h).start()
    gather(1 - parity, (far + side) & 3)
    for s in range(3):
        partial_image((zp + 3 - s) & 7, part_a)
        partial_image((zp + 5 + s) & 7, part_b)
        for h in range(4):
            rows, lanes = PIECES[h]
            for k, (part, send, got, copy) in enumerate(
                ((part_a, send_a, recv_a, copy_a), (part_b, send_b, recv_b, copy_b))
            ):
                total = part[rows, lanes]
                if s > 0:
                    if s == 1 and h // 2 == k:
                        copy_far(k, h).wait_recv()
                        total = total + recv_f[rows, lanes].astype(F32)
                    copy(s - 1, h).wait_recv()
                    total = total + got[s - 1, rows, lanes].astype(F32)
                send[s, rows, lanes] = total.astype(BF16)
                copy(s, h).start()
        if s == 0:
            gather(1 - parity, (far + 2) & 3)
            gather(1 - parity, (far - side) & 3)
    partial_image(zp, part_a)

    top = lax.broadcasted_iota(jnp.int32, (8, 128), 0) < 4
    turns = {}
    for q in range(4):
        labels = jnp.broadcast_to(group_ref[q:q + 1, :], (8, 128))
        for pair in range(2):
            angle = jnp.zeros((8, 128), F32)
            t = zp * 4 + pair * 2
            for n in range(16):
                angle = jnp.where(labels == n, jnp.where(top, error_ref[n, t], error_ref[n, t + 1]), angle)
            turns[q, pair] = unit_root(angle * (1.0 / TWO_PI))

    for h in range(4):
        rows, lanes = PIECES[h]
        copy_a(2, h).wait_recv()
        copy_b(2, h).wait_recv()
        part_a[rows, lanes] = (
            part_a[rows, lanes] + recv_a[2, rows, lanes].astype(F32) + recv_b[2, rows, lanes].astype(F32)
        )

    rights = []
    for vi in range(2):
        for q in range(4):
            for pair in range(2):
                row, at = vi * 16 + pair * 8, q * 128
                i_re = part_a[row:row + 8, at:at + 128]
                i_im = part_a[row:row + 8, 512 + at:640 + at]
                c, s = turns[q, pair]
                rights.append(jnp.concatenate([i_re * c - i_im * s, i_re * s + i_im * c], axis=1))
    right = (jnp.concatenate(rights, axis=0) * (1.0 / 1024)).astype(BF16)
    mid[0:256, 0:128] = lax.dot_general(
        focus_ref[...], right, (((1,), (1,)), ((), ())), preferred_element_type=F32
    )
    for dw in (2, 1, 3, 0):
        w = (wx + dw) & 3
        blocks = []
        for i in range(8):
            at = pl.multiple_of((i // 4) * 128 + w * 32 + (i % 4) * 8, 8)
            blocks.append(mid[pl.ds(at, 8), 0:128])
        blocks = swap_bits(blocks, 3)
        for i in range(8):
            msg2[(i // 2) * 8 + w * 2 + i % 2] = blocks[i]
    for d in PEERS:
        where, _, index = peer(d)
        pltpu.make_async_remote_copy(
            src_ref=msg2.at[index], dst_ref=recv2.at[me], send_sem=sem_s2.at[0], recv_sem=sem_r2.at[0],
            device_id=where, device_id_type=MESH,
        ).start()
    recv2[me] = msg2[py * 8 + wx * 2 + zb]

    all_first.wait_send()
    for h in range(4):
        copy_far(h // 2, h).wait_send()
        for s in range(3):
            copy_a(s, h).wait_send()
            copy_b(s, h).wait_send()
    all_last = pltpu.make_async_remote_copy(
        src_ref=recv2.at[pl.ds(0, 63)], dst_ref=recv2.at[pl.ds(0, 63)], send_sem=sem_s2.at[0], recv_sem=sem_r2.at[0],
        device_id=peer(1)[0], device_id_type=MESH,
    )
    all_last.wait_recv()

    high = (lax.broadcasted_iota(jnp.int32, (8, 128), 1) & 4) != 0
    blocks = []
    for n in range(32):
        k = (n >> 2) * 8 + (n & 3)
        a, b = recv2[k], recv2[k + 4]
        even = jnp.where(high, pltpu.roll(b, 4, 1), a)
        odd = jnp.where(high, b, pltpu.roll(a, 124, 1))
        blocks.append(jnp.where(core == 0, even, odd))
    low = swap_bits_of(blocks, ((1, 1), (2, 2), (4, 8), (8, 16), (16, 32)))
    for i in range(32):
        ri, hi, unit_at = i // 16, (i // 4) % 4, i % 4
        at = ri * 512 + unit_at * 128
        out_ref[hi * 8:hi * 8 + 8, at:at + 128] = low[i]
    all_last.wait_send()


def swap_bits_of(blocks, pairs):
    blocks = list(blocks)
    lane = lax.broadcasted_iota(jnp.int32, blocks[0].shape, 1)
    for bit, shift in pairs:
        high = (lane & shift) != 0
        for i in range(len(blocks)):
            if i & bit == 0:
                a, b = blocks[i], blocks[i | bit]
                blocks[i] = jnp.where(high, pltpu.roll(b, shift, 1), a)
                blocks[i | bit] = jnp.where(high, b, pltpu.roll(a, 128 - shift, 1))
    return blocks


def body(raw_pulses, range_weight, visibility, offsets, doppler_rate, phase_error, row_groups):
    first, twist, second, focus = dft_tables()
    vmem = pl.BlockSpec(memory_space=pltpu.VMEM)
    hbm = pl.BlockSpec(memory_space=pltpu.HBM)
    dma = pltpu.SemaphoreType.DMA
    focused = pl.pallas_call(
        image_kernel,
        out_shape=jax.ShapeDtypeStruct((32, 1024), F32),
        in_specs=[hbm] * 11,
        out_specs=vmem,
        scratch_shapes=[
            pltpu.SMEM((32,), jnp.int32),
            pltpu.SMEM((16, 32), F32),
            pltpu.VMEM((2, 16, 8192), F32),
            pltpu.VMEM((64, 128), F32),
            pltpu.VMEM((32, 512), jnp.int32),
            pltpu.VMEM((32, 512), jnp.int32),
            pltpu.VMEM((4, 128), jnp.int32),
            pltpu.VMEM((1024, 1024), BF16),
            pltpu.VMEM((2, 64, 128), F32),
            pltpu.VMEM((128, 256), BF16),
            pltpu.VMEM((256, 256), BF16),
            dma((11,)),
            pltpu.VMEM((1024, 256), BF16),
            pltpu.VMEM((1024, 256), F32),
            pltpu.VMEM((2048, 256), BF16),
            pltpu.VMEM((64, 32, 128), BF16),
            pltpu.VMEM((64, 32, 128), BF16),
            pltpu.VMEM((8, 2, 512, 256), BF16),
            pltpu.VMEM((32, 64, 128), BF16),
            pltpu.VMEM((32, 128, 1024), BF16),
            pltpu.VMEM((32, 4, 16, 128), F32),
            pltpu.VMEM((32, 1024), F32),
            pltpu.VMEM((32, 1024), F32),
            pltpu.VMEM((3, 32, 1024), BF16),
            pltpu.VMEM((3, 32, 1024), BF16),
            pltpu.VMEM((3, 32, 1024), BF16),
            pltpu.VMEM((3, 32, 1024), BF16),
            pltpu.VMEM((32, 1024), BF16),
            pltpu.VMEM((32, 1024), BF16),
            pltpu.VMEM((32, 8, 128), F32),
            pltpu.VMEM((64, 8, 128), F32),
            dma((1,)), dma((2,)),
            dma((3, 4)), dma((3, 4)), dma((3, 4)), dma((3, 4)),
            dma((4,)), dma((4,)),
            dma((1,)), dma((1,)),
        ],
        compiler_params=pltpu.CompilerParams(
            collective_id=0, has_side_effects=True, vmem_limit_bytes=62 * 2**20
        ),
    )(
        doppler_rate, phase_error.T, raw_pulses, range_weight.reshape(64, 128), offsets, visibility,
        row_groups.reshape(4, 128), jnp.asarray(first), jnp.asarray(twist), jnp.asarray(second), jnp.asarray(focus),
    )
    return focused[None]


def solution(mesh):
    return jax.shard_map(
        body,
        mesh=mesh,
        in_specs=(P(None, ("pulse", "tile", "row"), None), P(), P(), P(), P(), P(), P()),
        out_specs=P("tile", ("pulse", "row"), None),
        check_vma=False,
    )
```
